32 devices in a mesh: cb: 4 (over y, x), tp: 8 (over z, core).
Axes of the slice: x: 2, y: 2, z: 4, core: 2. Of those that a mesh axis runs over, the one named last changes fastest.
Arguments:
- hidden_in: bfloat16 [128, 4096], P('cb', 'tp'), may hold values from -6 to 6
- norm_gain: bfloat16 [4096], P('tp'), may hold values from 0.25 to 1.75
- w_qkv: bfloat16 [3, 4096, 4096], P(None, None, 'tp'), may hold values from -0.0625 to 0.0625
- w_out: bfloat16 [4096, 4096], P('tp'), may hold values from -0.09375 to 0.09375
- cache_keys: bfloat16 [128, 64, 4096], P(('cb', 'tp')), may hold values from -6 to 6
- cache_values: bfloat16 [128, 64, 4096], P(('cb', 'tp')), may hold values from -6 to 6
- lengths: int32 [128], P(('cb', 'tp')), may hold values from 2 to 64, as said below
- tokens: int32 [128, 8], P(None, 'cb'), may hold values from 0 to 2047
- w_in: bfloat16 [8, 4096, 1024], P('cb', 'tp'), may hold values from -0.09375 to 0.09375
- embed: bfloat16 [8, 2048, 1024], P('cb', None, 'tp'), may hold values from -6 to 6
- depth_gain: bfloat16 [8, 1024], P('cb'), may hold values from 0.25 to 1.75
- w_gate_up: bfloat16 [8, 2, 1024, 2816], P('cb', None, None, 'tp'), may hold values from -0.1875 to 0.1875
- w_down: bfloat16 [8, 2816, 1024], P('cb', 'tp'), may hold values from -0.109375 to 0.109375
Outputs:
- temporal_out: bfloat16 [128, 4096], P('cb', 'tp')
- depth_out: bfloat16 [8, 128, 1024], P('cb', None, 'tp')
The draws below stay inside these ranges and needn't reach their ends.
Inputs may be any that keep to these rules, and one draw needn't show every extreme that they name: `lengths`: number of live cache slots of each stream-beam; some row has all 64.
All inputs are finite; a program needn't handle non-finite values.
Results may differ from the reference program's by a relative error of at most 0.009.
Values may be sent and summed in bfloat16 or wider, within the bound.
A program may use at most 64 MiB of HBM per device.

```python
import math
import jax
import jax.numpy as jnp
from jax import lax

D = 4096
HEADS = 32
HEAD_DIM = 128
DD = 1024
FD = 2816
CARD = 2048
NCB = 8
CACHE = 64
ROWS = 128


def draw_lengths(key, part):
    key = jax.random.fold_in(key, 7)
    drawn = jax.random.randint(key, (ROWS,), 2, CACHE + 1, dtype=jnp.int32)
    return drawn.at[0].set(CACHE)


def draw_hidden_in(key, part):
    key = jax.random.fold_in(key, 11)
    key_drawn = jax.random.fold_in(key, 0)
    drawn = jnp.clip(jax.random.normal(key_drawn, (ROWS, D), jnp.float32), -6.0, 6.0)
    return drawn.astype(jnp.bfloat16)


def draw_w_qkv(key, part):
    key = jax.random.fold_in(key, 12)
    drawn = jnp.clip(jax.random.normal(key, (3, D, D), jnp.float32), -3.98, 3.98) / math.sqrt(D)
    return drawn.astype(jnp.bfloat16)


def draw_cache_keys(key, part):
    key = jax.random.fold_in(key, 13)
    drawn = jnp.clip(jax.random.normal(key, (ROWS, CACHE, D), jnp.float32), -6.0, 6.0)
    return drawn.astype(jnp.bfloat16)


def plant(values, rng, low, high):
    shape = values.shape
    place = [jax.random.randint(jax.random.fold_in(rng, axis), (), 0, shape[axis]) for axis in range(len(shape))]
    values = values.at[tuple(place)].set(low)
    longest = shape.index(max(shape))
    place[longest] = (place[longest] + 1) % shape[longest]
    return values.at[tuple(place)].set(high)


def level_of(stream_key, dims, cuts, least, high):
    def one(axis_at, blocks):
        draws = jax.random.uniform(jax.random.fold_in(jax.random.fold_in(stream_key, 6), axis_at), (blocks,), jnp.float32, least / len(cuts), high / len(cuts))
        return jnp.repeat(jnp.exp(draws), dims[axis_at] // blocks).reshape((-1,) + (1,) * (len(dims) - axis_at - 1))

    level = one(*cuts[0])
    for cut in cuts[1:]:
        level = level * one(*cut)
    return level


def centred(key, dims, width, most, cuts=(), kind=jnp.bfloat16):
    entries = width * jax.random.normal(key, dims, jnp.float32)
    if cuts:
        entries = entries * level_of(key, dims, cuts, -0.22, 0.18)
    return jnp.clip(entries, -most, most).astype(kind)


def setup_inputs(seed: int = 0) -> dict:
    splits = jax.random.split(jax.random.key(seed), 14)
    hidden_in = draw_hidden_in(jax.random.fold_in(splits[13], 71), 0)
    norm_gain = jnp.clip(1.0 + 0.15 * jax.random.normal(splits[1], (D,), jnp.float32), 0.25, 1.75).astype(jnp.bfloat16)
    w_qkv = draw_w_qkv(jax.random.fold_in(splits[13], 71), 0)
    w_out = centred(splits[3], (D, D), D ** -0.5, 0.09375, ((0, 8),))
    cache_keys = draw_cache_keys(jax.random.fold_in(splits[13], 71), 0)
    cache_values = centred(splits[5], (ROWS, CACHE, D), 1.0, 6.0, ((0, 32),))
    lengths = draw_lengths(jax.random.fold_in(splits[13], 71), 0)
    tokens = plant(jax.random.randint(splits[7], (ROWS, NCB), 0, CARD), jax.random.fold_in(splits[7], 1), 0, CARD - 1).astype(jnp.int32)
    w_in = centred(splits[8], (NCB, D, DD), D ** -0.5, 0.09375, ((0, 4), (1, 8)))
    embed = centred(splits[9], (NCB, CARD, DD), 1.0, 6.0, ((0, 4), (2, 8)))
    depth_gain = jnp.clip(1.0 + 0.15 * jax.random.normal(splits[10], (NCB, DD), jnp.float32), 0.25, 1.75).astype(jnp.bfloat16)
    w_gate_up = centred(splits[11], (NCB, 2, DD, FD), DD ** -0.5, 0.1875, ((0, 4), (3, 8)))
    w_down = centred(splits[12], (NCB, FD, DD), FD ** -0.5, 0.109375, ((0, 4), (1, 8)))
    return dict(hidden_in=hidden_in, norm_gain=norm_gain, w_qkv=w_qkv, w_out=w_out, cache_keys=cache_keys, cache_values=cache_values, lengths=lengths, tokens=tokens, w_in=w_in, embed=embed, depth_gain=depth_gain, w_gate_up=w_gate_up, w_down=w_down)


eps = 1e-05

def attend_block(args):
    query, key_new, value_new, keys, values, lens = args
    rows = query.shape[0]
    scale = 1.0 / math.sqrt(HEAD_DIM)
    query_h = query.astype(jnp.float32).reshape(rows, HEADS, HEAD_DIM)
    keys_h = keys.astype(jnp.float32).reshape(rows, CACHE, HEADS, HEAD_DIM)
    values_h = values.astype(jnp.float32).reshape(rows, CACHE, HEADS, HEAD_DIM)
    scores = jnp.einsum('rhe,rphe->rhp', query_h, keys_h) * scale
    live = jnp.arange(CACHE)[None, None, :] < lens[:, None, None]
    scores = jnp.where(live, scores, -1e+30)
    fresh = lax.optimization_barrier(jnp.sum(query_h * key_new.astype(jnp.float32).reshape(rows, HEADS, HEAD_DIM), axis=-1)) * scale
    top = jnp.maximum(lax.optimization_barrier(jnp.max(scores, axis=-1)), fresh)
    weights = jnp.exp(scores - top[..., None])
    weight_new = jnp.exp(fresh - top)
    total = lax.optimization_barrier(jnp.sum(weights, axis=-1)) + weight_new
    probs = (weights / total[..., None]).astype(jnp.bfloat16)
    prob_new = (weight_new / total).astype(jnp.bfloat16)
    mixed = jnp.einsum('rhp,rphe->rhe', probs.astype(jnp.float32), values_h)
    mixed = mixed + prob_new.astype(jnp.float32)[..., None] * value_new.astype(jnp.float32).reshape(rows, HEADS, HEAD_DIM)
    return mixed.reshape(rows, D).astype(jnp.bfloat16)

def reference(hidden_in, norm_gain, w_qkv, w_out, cache_keys, cache_values, lengths, tokens, w_in, embed, depth_gain, w_gate_up, w_down):
    hid32 = hidden_in.astype(jnp.float32)
    mean_sq = lax.optimization_barrier(jnp.mean(hid32 * hid32, axis=1))
    normed = (hid32 * lax.rsqrt(mean_sq + eps)[:, None] * norm_gain.astype(jnp.float32)).astype(jnp.bfloat16)
    qkv = jnp.einsum('rd,idf->rif', normed.astype(jnp.float32), w_qkv.astype(jnp.float32)).astype(jnp.bfloat16)
    block = math.gcd(ROWS, 64)
    count = ROWS // block
    attended = lax.map(attend_block, (qkv[:, 0].reshape(count, block, D), qkv[:, 1].reshape(count, block, D), qkv[:, 2].reshape(count, block, D), cache_keys.reshape(count, block, CACHE, D), cache_values.reshape(count, block, CACHE, D), lengths.reshape(count, block)))
    attended = attended.reshape(ROWS, D)
    temporal_out = (hid32 + jnp.dot(attended, w_out, preferred_element_type=jnp.float32)).astype(jnp.bfloat16)
    results = []
    for step in range(NCB):
        before = (step - 1) % NCB
        token_rows = embed[before][tokens[:, before]].astype(jnp.float32)
        x_step = jnp.dot(temporal_out, w_in[step], preferred_element_type=jnp.float32) + token_rows
        mean_d = lax.optimization_barrier(jnp.mean(x_step * x_step, axis=1))
        xn_step = (x_step * lax.rsqrt(mean_d + eps)[:, None] * depth_gain[step].astype(jnp.float32)).astype(jnp.bfloat16)
        gate = jnp.dot(xn_step, w_gate_up[step, 0], preferred_element_type=jnp.float32)
        upper = jnp.dot(xn_step, w_gate_up[step, 1], preferred_element_type=jnp.float32)
        act = (jax.nn.silu(gate) * upper).astype(jnp.bfloat16)
        results.append((x_step + jnp.dot(act, w_down[step], preferred_element_type=jnp.float32)).astype(jnp.bfloat16))
    return (temporal_out, jnp.stack(results))
```

```python
import functools
import math

import jax
import jax.numpy as jnp
from jax import lax
from jax.experimental import pallas as pl
from jax.experimental.pallas import tpu as pltpu
from jax.sharding import PartitionSpec as P

D = 4096
HEADS = 32
HEAD_DIM = 128
DD = 1024
CARD = 2048
CACHE = 64


eps = 1e-05


def from_behind(value, axis, steps):
    count = lax.axis_size(axis)
    pairs = [(source, (source + steps) % count) for source in range(count)]
    return lax.ppermute(value, axis, pairs)


def per_device(
    hidden_in,
    norm_gain,
    w_qkv,
    w_out,
    cache_keys,
    cache_values,
    lengths,
    tokens,
    w_in,
    embed,
    depth_gain,
    w_gate_up,
    w_down,
):
    width_tp = lax.axis_size("tp")
    group_rows, feat_loc = hidden_in.shape
    hid32 = hidden_in.astype(jnp.float32)
    sum_sq = lax.psum(jnp.sum(hid32 * hid32, axis=1), "tp")
    normed = (hid32 * lax.rsqrt(sum_sq / D + eps)[:, None] * norm_gain.astype(jnp.float32)).astype(
        jnp.bfloat16
    )
    qkv = jnp.einsum(
        "rd,idf->rif",
        lax.all_gather(normed, "tp", axis=1, tiled=True),
        w_qkv,
        preferred_element_type=jnp.float32,
    ).astype(jnp.bfloat16)
    per_dev = group_rows // width_tp
    arrived = lax.all_to_all(
        qkv.reshape(width_tp, per_dev, 3, feat_loc), "tp", split_axis=0, concat_axis=3, tiled=True
    )
    arrived = arrived.reshape(per_dev, 3, D)
    scale = 1.0 / math.sqrt(HEAD_DIM)
    query_h = arrived[:, 0].reshape(per_dev, HEADS, HEAD_DIM)
    key_new = arrived[:, 1].reshape(per_dev, HEADS, HEAD_DIM)
    value_new = arrived[:, 2].reshape(per_dev, HEADS, HEAD_DIM)
    keys_h = cache_keys.reshape(per_dev, CACHE, HEADS, HEAD_DIM)
    values_h = cache_values.reshape(per_dev, CACHE, HEADS, HEAD_DIM)
    scores = (
        jnp.einsum("rhe,rphe->rhp", query_h, keys_h, preferred_element_type=jnp.float32) * scale
    )
    live = lax.broadcasted_iota(jnp.int32, (1, 1, CACHE), 2) < lengths[:, None, None]
    scores = jnp.where(live, scores, -1e30)
    fresh = jnp.sum(query_h.astype(jnp.float32) * key_new.astype(jnp.float32), axis=-1) * scale
    top = jnp.maximum(jnp.max(scores, axis=-1), fresh)
    weights = jnp.exp(scores - top[..., None])
    weight_new = jnp.exp(fresh - top)
    total = jnp.sum(weights, axis=-1) + weight_new
    probs = (weights / total[..., None]).astype(jnp.bfloat16)
    prob_new = (weight_new / total).astype(jnp.bfloat16)
    mixed = jnp.einsum("rhp,rphe->rhe", probs, values_h, preferred_element_type=jnp.float32)
    mixed = mixed + prob_new.astype(jnp.float32)[..., None] * value_new.astype(jnp.float32)
    attended = mixed.reshape(per_dev, width_tp, feat_loc).astype(jnp.bfloat16)
    returned = lax.all_to_all(attended, "tp", split_axis=1, concat_axis=0, tiled=True).reshape(
        group_rows, feat_loc
    )
    partial_value = jnp.dot(returned, w_out, preferred_element_type=jnp.float32)
    attn_sum = lax.psum_scatter(partial_value, "tp", scatter_dimension=1, tiled=True)
    temporal_out = (hid32 + attn_sum).astype(jnp.bfloat16)
    frame = lax.all_gather(temporal_out, "cb", axis=0, tiled=True)
    steps_here = w_in.shape[0]
    depth_loc = embed.shape[2]
    column_start = lax.axis_index("tp") * depth_loc
    codes = lax.broadcasted_iota(jnp.int32, (1, CARD), 1)
    embedded = []
    for local in range(steps_here):
        one_hot = (tokens[:, local][:, None] == codes).astype(jnp.bfloat16)
        embedded.append(
            jnp.dot(one_hot, embed[local], preferred_element_type=jnp.float32).astype(jnp.bfloat16)
        )
    carried = from_behind(embedded[steps_here - 1], "cb", 1)
    previous = [carried] + embedded[: steps_here - 1]
    results = []
    for local in range(steps_here):
        term = jnp.dot(frame, w_in[local], preferred_element_type=jnp.float32)
        gain_all = depth_gain[local].astype(jnp.float32)
        x_loc = lax.psum_scatter(term, "tp", scatter_dimension=1, tiled=True) + previous[
            local
        ].astype(jnp.float32)
        sum_d = lax.psum(jnp.sum(x_loc * x_loc, axis=1), "tp")
        gain_loc = lax.dynamic_slice_in_dim(gain_all, column_start, depth_loc, 0)
        xn_loc = (x_loc * lax.rsqrt(sum_d / DD + eps)[:, None] * gain_loc).astype(jnp.bfloat16)
        weights_step = w_gate_up[local]
        gate_up = jnp.einsum(
            "rd,idf->irf",
            lax.all_gather(xn_loc, "tp", axis=1, tiled=True),
            weights_step,
            preferred_element_type=jnp.float32,
        )
        act = (jax.nn.silu(gate_up[0]) * gate_up[1]).astype(jnp.bfloat16)
        down_term = jnp.dot(act, w_down[local], preferred_element_type=jnp.float32)
        down_sum = lax.psum_scatter(down_term, "tp", scatter_dimension=1, tiled=True)
        results.append((x_loc + down_sum).astype(jnp.bfloat16))
    return (temporal_out, jnp.stack(results))


MESH = pl.DeviceIdType.MESH
NORM, GAIN, CARRY, QKV, BACK, OUT, FRAME, XSUM, XN, DOWN = 0, 1, 2, 3, 4, 5, 6, 7, 9, 11
PHASES = 13


def frame_kernel(
    ntp,
    ncb,
    hid,
    gain,
    lengths,
    tokens,
    depth_gain,
    w_qkv,
    w_out,
    keys,
    values,
    w_in,
    embed,
    w_gu,
    w_down,
    out_t,
    out_d,
    vq,
    vo,
    vk,
    vv,
    vi,
    ve,
    vg,
    vd,
    hid_all,
    gain_all,
    normed,
    qkv_send,
    qkv_recv,
    att_send,
    att_recv,
    returned,
    o_send,
    o_recv,
    frame,
    emb,
    carried,
    part,
    x_send,
    x_recv,
    x_own,
    xn_all,
    d_send,
    d_recv,
    wsem,
    ssem,
    rsem,
):
    f32, bf16 = jnp.float32, jnp.bfloat16
    me = lax.axis_index("tp")
    grp = lax.axis_index("cb")
    rows, feat = hid.shape
    per_dev = rows // ntp
    heads = feat // HEAD_DIM
    blk = per_dev * heads
    steps = w_in.shape[0]
    drows = frame.shape[0] * rows // ntp
    dfeat = DD // ntp
    order = sorted(range(1, ntp), key=lambda i: abs(i - ntp // 2))

    weights = {}

    def load(name, source, target, index):
        copy = pltpu.make_async_copy(source, target, wsem.at[index])
        copy.start()
        weights[name] = copy

    for i in range(3):
        load(("q", i), w_qkv.at[i], vq.at[i], i)
    load("e", embed, ve, 3)

    sent = []

    def put(source, target, phase, i, axis, device):
        copy = pltpu.make_async_remote_copy(
            src_ref=source,
            dst_ref=target,
            send_sem=ssem.at[phase, i],
            recv_sem=rsem.at[phase, i],
            device_id={axis: device},
            device_id_type=MESH,
        )
        copy.start()
        sent.append(copy)
        return copy

    def tp_at(i):
        return lax.rem(me + i, ntp)

    def cb_at(i):
        return lax.rem(grp + i, ncb)

    barrier = pltpu.get_barrier_semaphore()
    for i in range(1, ntp):
        pl.semaphore_signal(barrier, inc=1, device_id={"tp": tp_at(i)}, device_id_type=MESH)
    for i in range(1, ncb):
        pl.semaphore_signal(barrier, inc=1, device_id={"cb": cb_at(i)}, device_id_type=MESH)

    gain32 = gain[...].astype(f32)
    gain_rows = [gain32[:, h * HEAD_DIM : (h + 1) * HEAD_DIM] for h in range(heads)]
    gain_rows.append(jnp.zeros((16 - heads, HEAD_DIM), f32))
    gain_all[me] = jnp.concatenate(gain_rows, axis=0).astype(bf16)
    hid_all[me] = hid[...]
    pl.semaphore_wait(barrier, ntp - 1 + ncb - 1)

    arriving = []
    for i in order:
        arriving.append(put(hid_all.at[me], hid_all.at[me], NORM, i, "tp", tp_at(i)))
        arriving.append(put(gain_all.at[me], gain_all.at[me], GAIN, i, "tp", tp_at(i)))

    weights["e"].wait()
    codes = lax.broadcasted_iota(jnp.int32, (tokens.shape[0], CARD), 1)
    for local in range(steps):
        one_hot = (tokens[:, local : local + 1] == codes).astype(f32).astype(bf16)
        emb[local] = jnp.dot(one_hot, ve[local], preferred_element_type=f32).astype(bf16)
    carry = put(emb.at[steps - 1], carried, CARRY, 1, "cb", cb_at(1))

    for copy in arriving:
        copy.wait_recv()
    load("k", keys, vk, 4)
    load("v", values, vv, 5)
    load("o", w_out, vo, 6)
    load("i", w_in, vi, 7)
    load("g", w_gu, vg, 8)
    load("d", w_down, vd, 9)

    total = jnp.zeros((rows, 1), f32)
    for s in range(ntp):
        piece = hid_all[s].astype(f32)
        total = total + jnp.sum(piece * piece, axis=1, keepdims=True)
    inv = lax.rsqrt(total / D + eps)
    for s in range(ntp):
        piece = hid_all[s].astype(f32)
        gains = gain_all[s].astype(f32)
        for h in range(heads):
            cols = slice(h * HEAD_DIM, (h + 1) * HEAD_DIM)
            at = s * feat + h * HEAD_DIM
            normed[:, at : at + HEAD_DIM] = (
                piece[:, cols] * inv * gains[h : h + 1, :]
            ).astype(bf16)

    size = rows * heads
    place = lax.broadcasted_iota(jnp.int32, (size, size), 0)
    column = lax.broadcasted_iota(jnp.int32, (size, size), 1)
    source = ((place // per_dev) % heads) * rows + (place // blk) * per_dev + place % per_dev
    perm = (column == source).astype(f32).astype(bf16)
    for i in range(3):
        weights["q", i].wait()
        full = jnp.dot(normed[...], vq[i], preferred_element_type=f32).astype(bf16)
        stacked = jnp.concatenate(
            [full[:, h * HEAD_DIM : (h + 1) * HEAD_DIM] for h in range(heads)], axis=0
        )
        moved = jnp.dot(perm, stacked, preferred_element_type=f32).astype(bf16)
        qkv_send[:, i * blk : (i + 1) * blk, :] = moved.reshape(ntp, blk, HEAD_DIM)
    arriving = [
        put(qkv_send.at[tp_at(i)], qkv_recv.at[me], QKV, i, "tp", tp_at(i)) for i in order
    ]
    qkv_recv[me] = qkv_send[me]
    weights["k"].wait()
    weights["v"].wait()
    for copy in arriving:
        copy.wait_recv()

    scale = 1.0 / math.sqrt(HEAD_DIM)
    slots = per_dev * CACHE
    row = lax.broadcasted_iota(jnp.int32, (blk, slots), 0)
    col = lax.broadcasted_iota(jnp.int32, (blk, slots), 1)
    count = jnp.zeros((blk, slots), jnp.int32)
    for r in range(per_dev):
        count = jnp.where(col // CACHE == r, lengths[r], count)
    live = (row % per_dev == col // CACHE) & (col % CACHE < count)
    head_of = lax.broadcasted_iota(jnp.int32, (blk, HEAD_DIM), 0) // per_dev
    for s in range(ntp):
        query = qkv_recv[s, 0:blk, :].astype(f32)
        key_new = qkv_recv[s, blk : 2 * blk, :].astype(f32)
        value_new = qkv_recv[s, 2 * blk : 3 * blk, :].astype(f32)
        spread = jnp.concatenate(
            [jnp.where(head_of == h, query, 0.0) for h in range(heads)], axis=1
        ).astype(bf16)
        cols = slice(s * feat, (s + 1) * feat)
        old_keys = vk[:, :, cols].reshape(slots, feat)
        scores = (
            lax.dot_general(
                spread, old_keys, (((1,), (1,)), ((), ())), preferred_element_type=f32
            )
            * scale
        )
        scores = jnp.where(live, scores, -1e30)
        fresh = jnp.sum(query * key_new, axis=1, keepdims=True) * scale
        top = jnp.maximum(jnp.max(scores, axis=1, keepdims=True), fresh)
        weight = jnp.exp(scores - top)
        weight_new = jnp.exp(fresh - top)
        norm = jnp.sum(weight, axis=1, keepdims=True) + weight_new
        probs = (weight / norm).astype(bf16)
        prob_new = (weight_new / norm).astype(bf16).astype(f32)
        old_values = vv[:, :, cols].reshape(slots, feat)
        wide = jnp.dot(probs, old_values, preferred_element_type=f32)
        mixed = prob_new * value_new
        for h in range(heads):
            mixed = mixed + jnp.where(
                head_of == h, wide[:, h * HEAD_DIM : (h + 1) * HEAD_DIM], 0.0
            )
        att_send[s] = mixed.astype(bf16)
    arriving = [
        put(att_send.at[tp_at(i)], att_recv.at[me], BACK, i, "tp", tp_at(i)) for i in order
    ]
    att_recv[me] = att_send[me]
    for copy in arriving:
        copy.wait_recv()
    gathered = att_recv[...].reshape(ntp * blk, HEAD_DIM)
    place = lax.broadcasted_iota(jnp.int32, (rows, ntp * blk), 0)
    column = lax.broadcasted_iota(jnp.int32, (rows, ntp * blk), 1)
    for h in range(heads):
        source = (place // per_dev) * blk + h * per_dev + place % per_dev
        pick = (column == source).astype(f32).astype(bf16)
        returned[:, h * HEAD_DIM : (h + 1) * HEAD_DIM] = jnp.dot(
            pick, gathered, preferred_element_type=f32
        ).astype(bf16)

    weights["o"].wait()
    arriving = []
    for i in order + [0]:
        cols = pl.ds(pl.multiple_of(tp_at(i) * feat, feat), feat)
        term = jnp.dot(returned[...], vo[:, cols], preferred_element_type=f32)
        if i == 0:
            attn = term
        else:
            o_send[i] = term.astype(bf16)
            arriving.append(put(o_send.at[i], o_recv.at[i], OUT, i, "tp", tp_at(i)))
    for copy in arriving:
        copy.wait_recv()
    for i in range(1, ntp):
        attn = attn + o_recv[i].astype(f32)
    temporal = (hid[...].astype(f32) + attn).astype(bf16)
    out_t[...] = temporal
    frame[grp] = temporal

    arriving = [
        put(frame.at[grp], frame.at[grp], FRAME, i, "cb", cb_at(i)) for i in range(1, ncb)
    ]
    weights["i"].wait()
    carry.wait_recv()
    for copy in arriving:
        copy.wait_recv()
    lhs = frame[...].reshape(ncb * rows, feat)

    arriving = []
    own_cols = pl.ds(pl.multiple_of(me * dfeat, dfeat), dfeat)
    for local in range(steps):
        part[...] = jnp.dot(lhs, vi[local], preferred_element_type=f32)
        before = carried[...] if local == 0 else emb[local - 1]
        part[:, own_cols] = part[:, own_cols] + before.astype(f32)
        x_send[local] = part[...].astype(bf16).reshape(ntp, drows, DD)
        arriving.append(
            [
                put(
                    x_send.at[local, tp_at(i)], x_recv.at[local, i], XSUM + local, i, "tp", tp_at(i)
                )
                for i in order
            ]
        )
        own_rows = pl.ds(pl.multiple_of(me * drows, drows), drows)
        x_own[local] = part[own_rows, :]
    gathers = []
    for local in range(steps):
        for copy in arriving[local]:
            copy.wait_recv()
        x = x_own[local]
        for i in range(1, ntp):
            x = x + x_recv[local, i].astype(f32)
        x_own[local] = x
        inv = lax.rsqrt(jnp.sum(x * x, axis=1, keepdims=True) / DD + eps)
        gains = depth_gain[local : local + 1, :].astype(f32)
        xn_all[local, me] = (x * inv * gains).astype(bf16)
        gathers.append(
            [
                put(xn_all.at[local, me], xn_all.at[local, me], XN + local, i, "tp", tp_at(i))
                for i in order
            ]
        )

    weights["g"].wait()
    weights["d"].wait()
    arriving = []
    for local in range(steps):
        for copy in gathers[local]:
            copy.wait_recv()
        lhs = xn_all[local].reshape(ntp * drows, DD)
        gate = jnp.dot(lhs, vg[local, 0], preferred_element_type=f32)
        upper = jnp.dot(lhs, vg[local, 1], preferred_element_type=f32)
        act = (jax.nn.silu(gate) * upper).astype(bf16)
        part[...] = jnp.dot(act, vd[local], preferred_element_type=f32)
        own_rows = pl.ds(pl.multiple_of(me * drows, drows), drows)
        part[own_rows, :] = part[own_rows, :] + x_own[local]
        copies = []
        for i in order:
            cols = pl.ds(pl.multiple_of(tp_at(i) * dfeat, dfeat), dfeat)
            d_send[local, i] = part[:, cols].astype(bf16)
            copies.append(
                put(d_send.at[local, i], d_recv.at[local, i], DOWN + local, i, "tp", tp_at(i))
            )
        arriving.append(copies)
        out_d[local] = part[:, own_cols]
    for local in range(steps):
        for copy in arriving[local]:
            copy.wait_recv()
        y = out_d[local]
        for i in range(1, ntp):
            y = y + d_recv[local, i].astype(f32)
        out_d[local] = y
    for copy in sent:
        copy.wait_send()


def fits(mesh, hidden_in, w_in):
    ntp, ncb = mesh.shape["tp"], mesh.shape["cb"]
    rows, feat = hidden_in.shape[0] // ncb, hidden_in.shape[1] // ntp
    steps = w_in.shape[0] // ncb
    return (
        steps == 2
        and feat % HEAD_DIM == 0
        and feat // HEAD_DIM <= 16
        and rows % ntp == 0
        and (rows // ntp * (feat // HEAD_DIM)) % 16 == 0
        and (rows * ncb) % (16 * ntp) == 0
        and (DD // ntp) % 128 == 0
    )


def fused(
    hidden_in,
    norm_gain,
    w_qkv,
    w_out,
    cache_keys,
    cache_values,
    lengths,
    tokens,
    w_in,
    embed,
    depth_gain,
    w_gate_up,
    w_down,
):
    ntp, ncb = lax.axis_size("tp"), lax.axis_size("cb")
    f32, bf16 = jnp.float32, jnp.bfloat16
    rows, feat = hidden_in.shape
    blk = rows // ntp * (feat // HEAD_DIM)
    steps = w_in.shape[0]
    total_rows = rows * ncb
    drows, dfeat = total_rows // ntp, DD // ntp
    vmem = pl.BlockSpec(memory_space=pltpu.VMEM)
    hbm = pl.BlockSpec(memory_space=pl.ANY)
    big = [w_qkv, w_out, cache_keys, cache_values, w_in, embed, w_gate_up, w_down]
    scratch = [pltpu.VMEM(a.shape, a.dtype) for a in big] + [
        pltpu.VMEM((ntp, rows, feat), bf16),
        pltpu.VMEM((ntp, 16, HEAD_DIM), bf16),
        pltpu.VMEM((rows, D), bf16),
        pltpu.VMEM((ntp, 3 * blk, HEAD_DIM), bf16),
        pltpu.VMEM((ntp, 3 * blk, HEAD_DIM), bf16),
        pltpu.VMEM((ntp, blk, HEAD_DIM), bf16),
        pltpu.VMEM((ntp, blk, HEAD_DIM), bf16),
        pltpu.VMEM((rows, feat), bf16),
        pltpu.VMEM((ntp, rows, feat), bf16),
        pltpu.VMEM((ntp, rows, feat), bf16),
        pltpu.VMEM((ncb, rows, feat), bf16),
        pltpu.VMEM((steps, total_rows, dfeat), bf16),
        pltpu.VMEM((total_rows, dfeat), bf16),
        pltpu.VMEM((total_rows, DD), f32),
        pltpu.VMEM((steps, ntp, drows, DD), bf16),
        pltpu.VMEM((steps, ntp, drows, DD), bf16),
        pltpu.VMEM((steps, drows, DD), f32),
        pltpu.VMEM((steps, ntp, drows, DD), bf16),
        pltpu.VMEM((steps, ntp, total_rows, dfeat), bf16),
        pltpu.VMEM((steps, ntp, total_rows, dfeat), bf16),
        pltpu.SemaphoreType.DMA((10,)),
        pltpu.SemaphoreType.DMA((PHASES, ntp)),
        pltpu.SemaphoreType.DMA((PHASES, ntp)),
    ]
    temporal, depth = pl.pallas_call(
        functools.partial(frame_kernel, ntp, ncb),
        out_shape=(
            jax.ShapeDtypeStruct((rows, feat), bf16),
            jax.ShapeDtypeStruct((steps, total_rows, dfeat), f32),
        ),
        in_specs=[vmem, vmem, pl.BlockSpec(memory_space=pltpu.SMEM), vmem, vmem] + [hbm] * 8,
        out_specs=(vmem, vmem),
        scratch_shapes=scratch,
        compiler_params=pltpu.CompilerParams(
            collective_id=0, has_side_effects=True, vmem_limit_bytes=60 * 1024 * 1024
        ),
    )(
        hidden_in,
        norm_gain.reshape(1, feat),
        lengths,
        tokens,
        depth_gain,
        *big,
    )
    return temporal, depth.astype(bf16)


def solution(mesh):
    in_specs = (
        P("cb", "tp"),
        P("tp"),
        P(None, None, "tp"),
        P("tp", None),
        P(("cb", "tp"), None, None),
        P(("cb", "tp"), None, None),
        P(("cb", "tp")),
        P(None, "cb"),
        P("cb", "tp", None),
        P("cb", None, "tp"),
        P("cb", None),
        P("cb", None, None, "tp"),
        P("cb", "tp", None),
    )
    out_specs = (P("cb", "tp"), P("cb", None, "tp"))

    def run(*args):
        body = fused if fits(mesh, args[0], args[8]) else per_device
        return jax.shard_map(
            body, mesh=mesh, in_specs=in_specs, out_specs=out_specs, check_vma=False
        )(*args)

    return run
```

```python
import functools
import math

import jax
import jax.numpy as jnp
from jax import lax
from jax.experimental import pallas as pl
from jax.experimental.pallas import tpu as pltpu
from jax.sharding import PartitionSpec as P

D = 4096
HEADS = 32
HEAD_DIM = 128
DD = 1024
CARD = 2048
CACHE = 64


eps = 1e-05


def from_behind(value, axis, steps):
    count = lax.axis_size(axis)
    pairs = [(source, (source + steps) % count) for source in range(count)]
    return lax.ppermute(value, axis, pairs)


def per_device(
    hidden_in,
    norm_gain,
    w_qkv,
    w_out,
    cache_keys,
    cache_values,
    lengths,
    tokens,
    w_in,
    embed,
    depth_gain,
    w_gate_up,
    w_down,
):
    width_tp = lax.axis_size("tp")
    group_rows, feat_loc = hidden_in.shape
    hid32 = hidden_in.astype(jnp.float32)
    sum_sq = lax.psum(jnp.sum(hid32 * hid32, axis=1), "tp")
    normed = (hid32 * lax.rsqrt(sum_sq / D + eps)[:, None] * norm_gain.astype(jnp.float32)).astype(
        jnp.bfloat16
    )
    qkv = jnp.einsum(
        "rd,idf->rif",
        lax.all_gather(normed, "tp", axis=1, tiled=True),
        w_qkv,
        preferred_element_type=jnp.float32,
    ).astype(jnp.bfloat16)
    per_dev = group_rows // width_tp
    arrived = lax.all_to_all(
        qkv.reshape(width_tp, per_dev, 3, feat_loc), "tp", split_axis=0, concat_axis=3, tiled=True
    )
    arrived = arrived.reshape(per_dev, 3, D)
    scale = 1.0 / math.sqrt(HEAD_DIM)
    query_h = arrived[:, 0].reshape(per_dev, HEADS, HEAD_DIM)
    key_new = arrived[:, 1].reshape(per_dev, HEADS, HEAD_DIM)
    value_new = arrived[:, 2].reshape(per_dev, HEADS, HEAD_DIM)
    keys_h = cache_keys.reshape(per_dev, CACHE, HEADS, HEAD_DIM)
    values_h = cache_values.reshape(per_dev, CACHE, HEADS, HEAD_DIM)
    scores = (
        jnp.einsum("rhe,rphe->rhp", query_h, keys_h, preferred_element_type=jnp.float32) * scale
    )
    live = lax.broadcasted_iota(jnp.int32, (1, 1, CACHE), 2) < lengths[:, None, None]
    scores = jnp.where(live, scores, -1e30)
    fresh = jnp.sum(query_h.astype(jnp.float32) * key_new.astype(jnp.float32), axis=-1) * scale
    top = jnp.maximum(jnp.max(scores, axis=-1), fresh)
    weights = jnp.exp(scores - top[..., None])
    weight_new = jnp.exp(fresh - top)
    total = jnp.sum(weights, axis=-1) + weight_new
    probs = (weights / total[..., None]).astype(jnp.bfloat16)
    prob_new = (weight_new / total).astype(jnp.bfloat16)
    mixed = jnp.einsum("rhp,rphe->rhe", probs, values_h, preferred_element_type=jnp.float32)
    mixed = mixed + prob_new.astype(jnp.float32)[..., None] * value_new.astype(jnp.float32)
    attended = mixed.reshape(per_dev, width_tp, feat_loc).astype(jnp.bfloat16)
    returned = lax.all_to_all(attended, "tp", split_axis=1, concat_axis=0, tiled=True).reshape(
        group_rows, feat_loc
    )
    partial_value = jnp.dot(returned, w_out, preferred_element_type=jnp.float32)
    attn_sum = lax.psum_scatter(partial_value, "tp", scatter_dimension=1, tiled=True)
    temporal_out = (hid32 + attn_sum).astype(jnp.bfloat16)
    frame = lax.all_gather(temporal_out, "cb", axis=0, tiled=True)
    steps_here = w_in.shape[0]
    depth_loc = embed.shape[2]
    column_start = lax.axis_index("tp") * depth_loc
    codes = lax.broadcasted_iota(jnp.int32, (1, CARD), 1)
    embedded = []
    for local in range(steps_here):
        one_hot = (tokens[:, local][:, None] == codes).astype(jnp.bfloat16)
        embedded.append(
            jnp.dot(one_hot, embed[local], preferred_element_type=jnp.float32).astype(jnp.bfloat16)
        )
    carried = from_behind(embedded[steps_here - 1], "cb", 1)
    previous = [carried] + embedded[: steps_here - 1]
    results = []
    for local in range(steps_here):
        term = jnp.dot(frame, w_in[local], preferred_element_type=jnp.float32)
        gain_all = depth_gain[local].astype(jnp.float32)
        x_loc = lax.psum_scatter(term, "tp", scatter_dimension=1, tiled=True) + previous[
            local
        ].astype(jnp.float32)
        sum_d = lax.psum(jnp.sum(x_loc * x_loc, axis=1), "tp")
        gain_loc = lax.dynamic_slice_in_dim(gain_all, column_start, depth_loc, 0)
        xn_loc = (x_loc * lax.rsqrt(sum_d / DD + eps)[:, None] * gain_loc).astype(jnp.bfloat16)
        weights_step = w_gate_up[local]
        gate_up = jnp.einsum(
            "rd,idf->irf",
            lax.all_gather(xn_loc, "tp", axis=1, tiled=True),
            weights_step,
            preferred_element_type=jnp.float32,
        )
        act = (jax.nn.silu(gate_up[0]) * gate_up[1]).astype(jnp.bfloat16)
        down_term = jnp.dot(act, w_down[local], preferred_element_type=jnp.float32)
        down_sum = lax.psum_scatter(down_term, "tp", scatter_dimension=1, tiled=True)
        results.append((x_loc + down_sum).astype(jnp.bfloat16))
    return (temporal_out, jnp.stack(results))


MESH = pl.DeviceIdType.MESH
NORM, GAIN, CARRY, BACK, OUT, FRAME, XSUM, XN, DOWN, QKV = 0, 1, 2, 3, 4, 5, 6, 8, 10, 12
PHASES = 15


def frame_kernel(
    ntp,
    ncb,
    hid,
    gain,
    lengths,
    tokens,
    depth_gain,
    w_qkv,
    w_out,
    keys,
    values,
    w_in,
    embed,
    w_gu,
    w_down,
    out_t,
    out_d,
    vq,
    vo,
    vk,
    vv,
    vi,
    ve,
    vg,
    vd,
    hid_all,
    gain_all,
    normed,
    qkv_send,
    qkv_recv,
    att_send,
    att_recv,
    returned,
    o_twin,
    o_send,
    o_recv,
    frame,
    emb,
    carried,
    part,
    x_twin,
    x_send,
    x_recv,
    x_own,
    xn_all,
    d_twin,
    d_send,
    d_recv,
    wsem,
    ssem,
    rsem,
):
    f32, bf16 = jnp.float32, jnp.bfloat16
    me = lax.axis_index("tp")
    grp = lax.axis_index("cb")
    rows, feat = hid.shape
    per_dev = rows // ntp
    heads = feat // HEAD_DIM
    blk = per_dev * heads
    steps = w_in.shape[0]
    drows = frame.shape[0] * rows // ntp
    dfeat = DD // ntp
    order = sorted(range(1, ntp), key=lambda i: abs(i - ntp // 2))
    chips = ntp // 2
    core = lax.rem(me, 2)
    chip = lax.div(me, 2)
    twin = chip * 2 + 1 - core
    far = sorted(range(1, chips), key=lambda j: abs(j - chips // 2))

    weights = {}

    def load(name, source, target, index):
        copy = pltpu.make_async_copy(source, target, wsem.at[index])
        copy.start()
        weights[name] = copy

    for i in range(3):
        load(("q", i), w_qkv.at[i], vq.at[i], i)
    load("e", embed, ve, 3)

    sent = []

    def put(source, target, phase, i, axis, device):
        copy = pltpu.make_async_remote_copy(
            src_ref=source,
            dst_ref=target,
            send_sem=ssem.at[phase, i],
            recv_sem=rsem.at[phase, i],
            device_id={axis: device},
            device_id_type=MESH,
        )
        copy.start()
        sent.append(copy)
        return copy

    def tp_at(i):
        return lax.rem(me + i, ntp)

    def cb_at(i):
        return lax.rem(grp + i, ncb)

    def same_core(j):
        return lax.rem(chip + j, chips) * 2 + core

    def share(buffers, phases):
        direct = [
            [put(b.at[me], b.at[me], p, j, "tp", same_core(j)) for b, p in zip(buffers, phases)]
            for j in far
        ]
        passed = [put(b.at[me], b.at[me], p, chips, "tp", twin) for b, p in zip(buffers, phases)]
        return direct, passed

    def pass_on(buffers, phases, state):
        direct, passed = state
        for j, copies in zip(far, direct):
            origin = same_core(chips - j)
            for b, p, copy in zip(buffers, phases, copies):
                copy.wait_recv()
                passed.append(put(b.at[origin], b.at[origin], p, chips + j, "tp", twin))
        return passed

    barrier = pltpu.get_barrier_semaphore()
    for i in range(1, ntp):
        pl.semaphore_signal(barrier, inc=1, device_id={"tp": tp_at(i)}, device_id_type=MESH)
    for i in range(1, ncb):
        pl.semaphore_signal(barrier, inc=1, device_id={"cb": cb_at(i)}, device_id_type=MESH)

    gain32 = gain[...].reshape(1, feat).astype(f32)
    gain_rows = [gain32[:, h * HEAD_DIM : (h + 1) * HEAD_DIM] for h in range(heads)]
    gain_rows.append(jnp.zeros((16 - heads, HEAD_DIM), f32))
    gain_all[me] = jnp.concatenate(gain_rows, axis=0).astype(bf16)
    hid_all[me] = hid[...]
    pl.semaphore_wait(barrier, ntp - 1 + ncb - 1)

    shared = share([hid_all, gain_all], [NORM, GAIN])

    weights["e"].wait()
    codes = lax.broadcasted_iota(jnp.int32, (tokens.shape[1], CARD), 1)
    for local in range(steps):
        spread = jnp.broadcast_to(tokens[local : local + 1, :], (128, tokens.shape[1]))
        chosen = jnp.transpose(spread)[:, 0:1]
        one_hot = (chosen == codes).astype(f32).astype(bf16)
        emb[local] = jnp.dot(one_hot, ve[local], preferred_element_type=f32).astype(bf16)
    carry = put(emb.at[steps - 1], carried, CARRY, 1, "cb", cb_at(1))

    for copy in pass_on([hid_all, gain_all], [NORM, GAIN], shared):
        copy.wait_recv()
    load("k", keys, vk, 4)
    load("v", values, vv, 5)
    load("o", w_out, vo, 6)
    load("i", w_in, vi, 7)
    load("g", w_gu, vg, 8)
    load("d", w_down, vd, 9)

    total = jnp.zeros((rows, 1), f32)
    for s in range(ntp):
        piece = hid_all[s].astype(f32)
        total = total + jnp.sum(piece * piece, axis=1, keepdims=True)
    inv = lax.rsqrt(total / D + eps)
    for s in range(ntp):
        piece = hid_all[s].astype(f32)
        gains = gain_all[s].astype(f32)
        for h in range(heads):
            cols = slice(h * HEAD_DIM, (h + 1) * HEAD_DIM)
            at = s * feat + h * HEAD_DIM
            normed[:, at : at + HEAD_DIM] = (
                piece[:, cols] * inv * gains[h : h + 1, :]
            ).astype(bf16)

    size = rows * heads
    place = lax.broadcasted_iota(jnp.int32, (size, size), 0)
    column = lax.broadcasted_iota(jnp.int32, (size, size), 1)
    source = ((place // per_dev) % heads) * rows + (place // blk) * per_dev + place % per_dev
    perm = (column == source).astype(f32).astype(bf16)
    arriving = []
    for i in range(3):
        weights["q", i].wait()
        full = jnp.dot(normed[...], vq[i], preferred_element_type=f32).astype(bf16)
        stacked = jnp.concatenate(
            [full[:, h * HEAD_DIM : (h + 1) * HEAD_DIM] for h in range(heads)], axis=0
        )
        moved = jnp.dot(perm, stacked, preferred_element_type=f32).astype(bf16)
        qkv_send[i] = moved.reshape(ntp, blk, HEAD_DIM)
        arriving += [
            put(qkv_send.at[i, tp_at(j)], qkv_recv.at[i, me], QKV + i, j, "tp", tp_at(j))
            for j in order
        ]
        qkv_recv[i, me] = qkv_send[i, me]
    weights["k"].wait()
    weights["v"].wait()
    for copy in arriving:
        copy.wait_recv()

    scale = 1.0 / math.sqrt(HEAD_DIM)
    slots = per_dev * CACHE
    row = lax.broadcasted_iota(jnp.int32, (blk, slots), 0)
    col = lax.broadcasted_iota(jnp.int32, (blk, slots), 1)
    count = jnp.zeros((blk, slots), jnp.int32)
    for r in range(per_dev):
        count = jnp.where(col // CACHE == r, lengths[r], count)
    live = (row % per_dev == col // CACHE) & (col % CACHE < count)
    head_of = lax.broadcasted_iota(jnp.int32, (blk, HEAD_DIM), 0) // per_dev
    for s in range(ntp):
        query = qkv_recv[0, s].astype(f32)
        key_new = qkv_recv[1, s].astype(f32)
        value_new = qkv_recv[2, s].astype(f32)
        spread = jnp.concatenate(
            [jnp.where(head_of == h, query, 0.0) for h in range(heads)], axis=1
        ).astype(bf16)
        cols = slice(s * feat, (s + 1) * feat)
        old_keys = vk[:, :, cols].reshape(slots, feat)
        scores = (
            lax.dot_general(
                spread, old_keys, (((1,), (1,)), ((), ())), preferred_element_type=f32
            )
            * scale
        )
        scores = jnp.where(live, scores, -1e30)
        fresh = jnp.sum(query * key_new, axis=1, keepdims=True) * scale
        top = jnp.maximum(jnp.max(scores, axis=1, keepdims=True), fresh)
        weight = jnp.exp(scores - top)
        weight_new = jnp.exp(fresh - top)
        norm = jnp.sum(weight, axis=1, keepdims=True) + weight_new
        probs = (weight / norm).astype(bf16)
        prob_new = (weight_new / norm).astype(bf16).astype(f32)
        old_values = vv[:, :, cols].reshape(slots, feat)
        wide = jnp.dot(probs, old_values, preferred_element_type=f32)
        mixed = prob_new * value_new
        for h in range(heads):
            mixed = mixed + jnp.where(
                head_of == h, wide[:, h * HEAD_DIM : (h + 1) * HEAD_DIM], 0.0
            )
        att_send[s] = mixed.astype(bf16)
    arriving = [
        put(att_send.at[tp_at(i)], att_recv.at[me], BACK, i, "tp", tp_at(i)) for i in order
    ]
    att_recv[me] = att_send[me]
    for copy in arriving:
        copy.wait_recv()
    gathered = att_recv[...].reshape(ntp * blk, HEAD_DIM)
    place = lax.broadcasted_iota(jnp.int32, (rows, ntp * blk), 0)
    column = lax.broadcasted_iota(jnp.int32, (rows, ntp * blk), 1)
    for h in range(heads):
        source = (place // per_dev) * blk + h * per_dev + place % per_dev
        pick = (column == source).astype(f32).astype(bf16)
        returned[:, h * HEAD_DIM : (h + 1) * HEAD_DIM] = jnp.dot(
            pick, gathered, preferred_element_type=f32
        ).astype(bf16)

    weights["o"].wait()

    def projected(device):
        cols = pl.ds(pl.multiple_of(device * feat, feat), feat)
        return jnp.dot(returned[...], vo[:, cols], preferred_element_type=f32)

    for z in range(chips):
        o_twin[0, z] = projected(2 * z + 1 - core).astype(bf16)
    merged = put(o_twin.at[0], o_twin.at[1], OUT, 0, "tp", twin)
    mine = [projected(same_core(j)) for j in far + [0]]
    merged.wait_recv()
    arriving = []
    for j, term in zip(far, mine):
        o_send[j] = (term + o_twin[1, lax.rem(chip + j, chips)].astype(f32)).astype(bf16)
        arriving.append(put(o_send.at[j], o_recv.at[j], OUT, j, "tp", same_core(j)))
    attn = mine[-1] + o_twin[1, chip].astype(f32)
    for j, copy in zip(far, arriving):
        copy.wait_recv()
        attn = attn + o_recv[j].astype(f32)
    temporal = (hid[...].astype(f32) + attn).astype(bf16)
    out_t[...] = temporal
    frame[grp] = temporal

    arriving = [
        put(frame.at[grp], frame.at[grp], FRAME, i, "cb", cb_at(i)) for i in range(1, ncb)
    ]
    weights["i"].wait()
    carry.wait_recv()
    for copy in arriving:
        copy.wait_recv()
    lhs = frame[...].reshape(ncb * rows, feat)

    own_cols = pl.ds(pl.multiple_of(me * dfeat, dfeat), dfeat)

    def rows_of(device):
        return pl.ds(pl.multiple_of(device * drows, drows), drows)

    def cols_of(device):
        return pl.ds(pl.multiple_of(device * dfeat, dfeat), dfeat)

    merged = []
    for local in range(steps):
        part[local] = jnp.dot(lhs, vi[local], preferred_element_type=f32)
        before = carried[...] if local == 0 else emb[local - 1]
        part[local, :, own_cols] = part[local, :, own_cols] + before.astype(f32)
        for z in range(chips):
            x_twin[local, 0, z] = part[local, rows_of(2 * z + 1 - core), :].astype(bf16)
        merged.append(
            put(x_twin.at[local, 0], x_twin.at[local, 1], XSUM + local, 0, "tp", twin)
        )
    arriving = []
    for local in range(steps):
        merged[local].wait_recv()
        copies = []
        for j in far:
            x_send[local, j] = (
                part[local, rows_of(same_core(j)), :]
                + x_twin[local, 1, lax.rem(chip + j, chips)].astype(f32)
            ).astype(bf16)
            copies.append(
                put(x_send.at[local, j], x_recv.at[local, j], XSUM + local, j, "tp", same_core(j))
            )
        arriving.append(copies)
    gathers = []
    for local in range(steps):
        x = part[local, rows_of(me), :] + x_twin[local, 1, chip].astype(f32)
        for j, copy in zip(far, arriving[local]):
            copy.wait_recv()
            x = x + x_recv[local, j].astype(f32)
        x_own[local] = x
        inv = lax.rsqrt(jnp.sum(x * x, axis=1, keepdims=True) / DD + eps)
        gains = depth_gain[local : local + 1, :].astype(f32)
        xn_all[local, me] = (x * inv * gains).astype(bf16)
        gathers.append(share([xn_all.at[local]], [XN + local]))

    weights["g"].wait()
    weights["d"].wait()
    contract_last = (((1,), (1,)), ((), ()))
    for local in range(steps):
        gathers[local] = pass_on([xn_all.at[local]], [XN + local], gathers[local])
    merged, summed = [], []

    def send_down(local):
        merged[local].wait_recv()
        copies = []
        for j in far:
            d_send[local, j] = (
                part[local, :, cols_of(same_core(j))]
                + d_twin[local, 1, lax.rem(chip + j, chips)].astype(f32)
            ).astype(bf16)
            copies.append(
                put(d_send.at[local, j], d_recv.at[local, j], DOWN + local, j, "tp", same_core(j))
            )
        summed.append(copies)

    for local in range(steps):
        for copy in gathers[local]:
            copy.wait_recv()
        lhs = xn_all[local].reshape(ntp * drows, DD)
        gate = lax.dot_general(lhs, vg[local, 0], contract_last, preferred_element_type=f32)
        upper = lax.dot_general(lhs, vg[local, 1], contract_last, preferred_element_type=f32)
        act = (jax.nn.silu(gate) * upper).astype(bf16)
        part[local] = jnp.dot(act, vd[local], preferred_element_type=f32)
        part[local, rows_of(me), :] = part[local, rows_of(me), :] + x_own[local]
        for z in range(chips):
            d_twin[local, 0, z] = part[local, :, cols_of(2 * z + 1 - core)].astype(bf16)
        merged.append(
            put(d_twin.at[local, 0], d_twin.at[local, 1], DOWN + local, 0, "tp", twin)
        )
        if local:
            send_down(local - 1)
    send_down(steps - 1)
    for local in range(steps):
        y = part[local, :, own_cols] + d_twin[local, 1, chip].astype(f32)
        for j, copy in zip(far, summed[local]):
            copy.wait_recv()
            y = y + d_recv[local, j].astype(f32)
        out_d[local] = y.astype(out_d.dtype)
    for copy in sent:
        copy.wait_send()


def finish(temporal, depth, out_t, out_d):
    out_t[...] = temporal[...]
    out_d[...] = depth[...]


def fits(mesh, hidden_in, w_in):
    ntp, ncb = mesh.shape["tp"], mesh.shape["cb"]
    rows, feat = hidden_in.shape[0] // ncb, hidden_in.shape[1] // ntp
    steps = w_in.shape[0] // ncb
    return (
        steps == 2
        and ntp % 2 == 0
        and rows * ncb == 128
        and feat % HEAD_DIM == 0
        and feat // HEAD_DIM <= 16
        and rows % ntp == 0
        and (rows // ntp * (feat // HEAD_DIM)) % 16 == 0
        and (rows * ncb) % (16 * ntp) == 0
        and (DD // ntp) % 128 == 0
    )


def fused(
    hidden_in,
    norm_gain,
    w_qkv,
    w_out,
    cache_keys,
    cache_values,
    lengths,
    tokens,
    w_in,
    embed,
    depth_gain,
    w_gate_up,
    w_down,
):
    ntp, ncb = lax.axis_size("tp"), lax.axis_size("cb")
    f32, bf16 = jnp.float32, jnp.bfloat16
    rows, feat = hidden_in.shape
    blk = rows // ntp * (feat // HEAD_DIM)
    steps = w_in.shape[0]
    chips = ntp // 2
    total_rows = rows * ncb
    drows, dfeat = total_rows // ntp, DD // ntp
    vmem = pl.BlockSpec(memory_space=pltpu.VMEM)
    hbm = pl.BlockSpec(memory_space=pl.ANY)
    big = [w_qkv, w_out, cache_keys, cache_values, w_in, embed, jnp.swapaxes(w_gate_up, 2, 3), w_down]
    scratch = [pltpu.VMEM(a.shape, a.dtype) for a in big] + [
        pltpu.VMEM((ntp, rows, feat), bf16),
        pltpu.VMEM((ntp, 16, HEAD_DIM), bf16),
        pltpu.VMEM((rows, D), bf16),
        pltpu.VMEM((3, ntp, blk, HEAD_DIM), bf16),
        pltpu.VMEM((3, ntp, blk, HEAD_DIM), bf16),
        pltpu.VMEM((ntp, blk, HEAD_DIM), bf16),
        pltpu.VMEM((ntp, blk, HEAD_DIM), bf16),
        pltpu.VMEM((rows, feat), bf16),
        pltpu.VMEM((2, chips, rows, feat), bf16),
        pltpu.VMEM((chips, rows, feat), bf16),
        pltpu.VMEM((chips, rows, feat), bf16),
        pltpu.VMEM((ncb, rows, feat), bf16),
        pltpu.VMEM((steps, total_rows, dfeat), bf16),
        pltpu.VMEM((total_rows, dfeat), bf16),
        pltpu.VMEM((steps, total_rows, DD), f32),
        pltpu.VMEM((steps, 2, chips, drows, DD), bf16),
        pltpu.VMEM((steps, chips, drows, DD), bf16),
        pltpu.VMEM((steps, chips, drows, DD), bf16),
        pltpu.VMEM((steps, drows, DD), f32),
        pltpu.VMEM((steps, ntp, drows, DD), bf16),
        pltpu.VMEM((steps, 2, chips, total_rows, dfeat), bf16),
        pltpu.VMEM((steps, chips, total_rows, dfeat), bf16),
        pltpu.VMEM((steps, chips, total_rows, dfeat), bf16),
        pltpu.SemaphoreType.DMA((10,)),
        pltpu.SemaphoreType.DMA((PHASES, ntp)),
        pltpu.SemaphoreType.DMA((PHASES, ntp)),
    ]
    temporal, depth = pl.pallas_call(
        functools.partial(frame_kernel, ntp, ncb),
        out_shape=(
            jax.ShapeDtypeStruct((rows, feat), bf16),
            jax.ShapeDtypeStruct((steps, total_rows, dfeat), bf16),
        ),
        in_specs=[vmem, vmem, pl.BlockSpec(memory_space=pltpu.SMEM), vmem, vmem] + [hbm] * 8,
        out_specs=(vmem, vmem),
        scratch_shapes=scratch,
        compiler_params=pltpu.CompilerParams(
            collective_id=0, has_side_effects=True, vmem_limit_bytes=60 * 1024 * 1024
        ),
    )(
        hidden_in,
        norm_gain,
        lengths,
        tokens.T,
        depth_gain,
        *big,
    )
    return pl.pallas_call(
        finish,
        out_shape=(
            jax.ShapeDtypeStruct(temporal.shape, bf16),
            jax.ShapeDtypeStruct(depth.shape, bf16),
        ),
        in_specs=[vmem, vmem],
        out_specs=(vmem, vmem),
    )(temporal, depth)


def solution(mesh):
    in_specs = (
        P("cb", "tp"),
        P("tp"),
        P(None, None, "tp"),
        P("tp", None),
        P(("cb", "tp"), None, None),
        P(("cb", "tp"), None, None),
        P(("cb", "tp")),
        P(None, "cb"),
        P("cb", "tp", None),
        P("cb", None, "tp"),
        P("cb", None),
        P("cb", None, None, "tp"),
        P("cb", "tp", None),
    )
    out_specs = (P("cb", "tp"), P("cb", None, "tp"))

    def run(*args):
        body = fused if fits(mesh, args[0], args[8]) else per_device
        return jax.shard_map(
            body, mesh=mesh, in_specs=in_specs, out_specs=out_specs, check_vma=False
        )(*args)

    return run
```

```python
import functools
import math

import jax
import jax.numpy as jnp
from jax import lax
from jax.experimental import pallas as pl
from jax.experimental.pallas import tpu as pltpu
from jax.sharding import PartitionSpec as P

D = 4096
HEADS = 32
HEAD_DIM = 128
DD = 1024
CARD = 2048
CACHE = 64


eps = 1e-05


def from_behind(value, axis, steps):
    count = lax.axis_size(axis)
    pairs = [(source, (source + steps) % count) for source in range(count)]
    return lax.ppermute(value, axis, pairs)


def per_device(
    hidden_in,
    norm_gain,
    w_qkv,
    w_out,
    cache_keys,
    cache_values,
    lengths,
    tokens,
    w_in,
    embed,
    depth_gain,
    w_gate_up,
    w_down,
):
    width_tp = lax.axis_size("tp")
    group_rows, feat_loc = hidden_in.shape
    hid32 = hidden_in.astype(jnp.float32)
    sum_sq = lax.psum(jnp.sum(hid32 * hid32, axis=1), "tp")
    normed = (hid32 * lax.rsqrt(sum_sq / D + eps)[:, None] * norm_gain.astype(jnp.float32)).astype(
        jnp.bfloat16
    )
    qkv = jnp.einsum(
        "rd,idf->rif",
        lax.all_gather(normed, "tp", axis=1, tiled=True),
        w_qkv,
        preferred_element_type=jnp.float32,
    ).astype(jnp.bfloat16)
    per_dev = group_rows // width_tp
    arrived = lax.all_to_all(
        qkv.reshape(width_tp, per_dev, 3, feat_loc), "tp", split_axis=0, concat_axis=3, tiled=True
    )
    arrived = arrived.reshape(per_dev, 3, D)
    scale = 1.0 / math.sqrt(HEAD_DIM)
    query_h = arrived[:, 0].reshape(per_dev, HEADS, HEAD_DIM)
    key_new = arrived[:, 1].reshape(per_dev, HEADS, HEAD_DIM)
    value_new = arrived[:, 2].reshape(per_dev, HEADS, HEAD_DIM)
    keys_h = cache_keys.reshape(per_dev, CACHE, HEADS, HEAD_DIM)
    values_h = cache_values.reshape(per_dev, CACHE, HEADS, HEAD_DIM)
    scores = (
        jnp.einsum("rhe,rphe->rhp", query_h, keys_h, preferred_element_type=jnp.float32) * scale
    )
    live = lax.broadcasted_iota(jnp.int32, (1, 1, CACHE), 2) < lengths[:, None, None]
    scores = jnp.where(live, scores, -1e30)
    fresh = jnp.sum(query_h.astype(jnp.float32) * key_new.astype(jnp.float32), axis=-1) * scale
    top = jnp.maximum(jnp.max(scores, axis=-1), fresh)
    weights = jnp.exp(scores - top[..., None])
    weight_new = jnp.exp(fresh - top)
    total = jnp.sum(weights, axis=-1) + weight_new
    probs = (weights / total[..., None]).astype(jnp.bfloat16)
    prob_new = (weight_new / total).astype(jnp.bfloat16)
    mixed = jnp.einsum("rhp,rphe->rhe", probs, values_h, preferred_element_type=jnp.float32)
    mixed = mixed + prob_new.astype(jnp.float32)[..., None] * value_new.astype(jnp.float32)
    attended = mixed.reshape(per_dev, width_tp, feat_loc).astype(jnp.bfloat16)
    returned = lax.all_to_all(attended, "tp", split_axis=1, concat_axis=0, tiled=True).reshape(
        group_rows, feat_loc
    )
    partial_value = jnp.dot(returned, w_out, preferred_element_type=jnp.float32)
    attn_sum = lax.psum_scatter(partial_value, "tp", scatter_dimension=1, tiled=True)
    temporal_out = (hid32 + attn_sum).astype(jnp.bfloat16)
    frame = lax.all_gather(temporal_out, "cb", axis=0, tiled=True)
    steps_here = w_in.shape[0]
    depth_loc = embed.shape[2]
    column_start = lax.axis_index("tp") * depth_loc
    codes = lax.broadcasted_iota(jnp.int32, (1, CARD), 1)
    embedded = []
    for local in range(steps_here):
        one_hot = (tokens[:, local][:, None] == codes).astype(jnp.bfloat16)
        embedded.append(
            jnp.dot(one_hot, embed[local], preferred_element_type=jnp.float32).astype(jnp.bfloat16)
        )
    carried = from_behind(embedded[steps_here - 1], "cb", 1)
    previous = [carried] + embedded[: steps_here - 1]
    results = []
    for local in range(steps_here):
        term = jnp.dot(frame, w_in[local], preferred_element_type=jnp.float32)
        gain_all = depth_gain[local].astype(jnp.float32)
        x_loc = lax.psum_scatter(term, "tp", scatter_dimension=1, tiled=True) + previous[
            local
        ].astype(jnp.float32)
        sum_d = lax.psum(jnp.sum(x_loc * x_loc, axis=1), "tp")
        gain_loc = lax.dynamic_slice_in_dim(gain_all, column_start, depth_loc, 0)
        xn_loc = (x_loc * lax.rsqrt(sum_d / DD + eps)[:, None] * gain_loc).astype(jnp.bfloat16)
        weights_step = w_gate_up[local]
        gate_up = jnp.einsum(
            "rd,idf->irf",
            lax.all_gather(xn_loc, "tp", axis=1, tiled=True),
            weights_step,
            preferred_element_type=jnp.float32,
        )
        act = (jax.nn.silu(gate_up[0]) * gate_up[1]).astype(jnp.bfloat16)
        down_term = jnp.dot(act, w_down[local], preferred_element_type=jnp.float32)
        down_sum = lax.psum_scatter(down_term, "tp", scatter_dimension=1, tiled=True)
        results.append((x_loc + down_sum).astype(jnp.bfloat16))
    return (temporal_out, jnp.stack(results))


MESH = pl.DeviceIdType.MESH
NORM, GAIN, CARRY, BACK, OUT, FRAME, XSUM, XN, DOWN, QKV = 0, 1, 2, 3, 4, 5, 6, 8, 10, 12
PHASES = 15


def frame_kernel(
    ntp,
    ncb,
    hid,
    gain,
    lengths,
    tokens,
    depth_gain,
    w_qkv,
    w_out,
    keys,
    values,
    w_in,
    embed,
    w_gu,
    w_down,
    out_t,
    out_d,
    vq,
    vo,
    vk,
    vv,
    vi,
    ve,
    vg,
    vd,
    hid_all,
    gain_all,
    acc,
    qkv_send,
    qkv_recv,
    att_send,
    att_recv,
    returned,
    o_twin,
    o_send,
    o_recv,
    frame,
    emb,
    carried,
    part,
    x_twin,
    x_send,
    x_recv,
    x_own,
    xn_all,
    d_twin,
    d_send,
    d_recv,
    wsem,
    ssem,
    rsem,
):
    f32, bf16 = jnp.float32, jnp.bfloat16
    me = lax.axis_index("tp")
    grp = lax.axis_index("cb")
    rows, feat = hid.shape
    per_dev = rows // ntp
    heads = feat // HEAD_DIM
    blk = per_dev * heads
    steps = w_in.shape[0]
    drows = frame.shape[0] * rows // ntp
    dfeat = DD // ntp
    order = sorted(range(1, ntp), key=lambda i: abs(i - ntp // 2))
    chips = ntp // 2
    core = lax.rem(me, 2)
    chip = lax.div(me, 2)
    twin = chip * 2 + 1 - core
    far = sorted(range(1, chips), key=lambda j: abs(j - chips // 2))

    weights = {}

    def load(name, source, target, index):
        copy = pltpu.make_async_copy(source, target, wsem.at[index])
        copy.start()
        weights[name] = copy


    sent = []

    def put(source, target, phase, i, axis, device):
        copy = pltpu.make_async_remote_copy(
            src_ref=source,
            dst_ref=target,
            send_sem=ssem.at[phase, i],
            recv_sem=rsem.at[phase, i],
            device_id={axis: device},
            device_id_type=MESH,
        )
        copy.start()
        sent.append(copy)
        return copy

    def tp_at(i):
        return lax.rem(me + i, ntp)

    def cb_at(i):
        return lax.rem(grp + i, ncb)

    def same_core(j):
        return lax.rem(chip + j, chips) * 2 + core

    def share(buffers, phases):
        direct = [
            [put(b.at[me], b.at[me], p, j, "tp", same_core(j)) for b, p in zip(buffers, phases)]
            for j in far
        ]
        passed = [put(b.at[me], b.at[me], p, chips, "tp", twin) for b, p in zip(buffers, phases)]
        return direct, passed

    def pass_on(buffers, phases, state):
        direct, passed = state
        for j, copies in zip(far, direct):
            origin = same_core(chips - j)
            for b, p, copy in zip(buffers, phases, copies):
                copy.wait_recv()
                passed.append(put(b.at[origin], b.at[origin], p, chips + j, "tp", twin))
        return passed

    barrier = pltpu.get_barrier_semaphore()
    for i in range(1, ntp):
        pl.semaphore_signal(barrier, inc=1, device_id={"tp": tp_at(i)}, device_id_type=MESH)
    for i in range(1, ncb):
        pl.semaphore_signal(barrier, inc=1, device_id={"cb": cb_at(i)}, device_id_type=MESH)

    def part_of(device):
        return pl.ds(pl.multiple_of(device * feat, feat), feat)

    visits = [me, twin]
    visits += [same_core(chips - j) for j in far]
    visits += [same_core(chips - j) + 1 - 2 * core for j in far]
    for n, origin in enumerate(visits):
        load(
            ("q", n), w_qkv.at[:, part_of(origin), :], vq.at[:, part_of(origin), :], n
        )
    gain32 = gain[...].reshape(1, feat).astype(f32)
    gain_rows = [gain32[:, h * HEAD_DIM : (h + 1) * HEAD_DIM] for h in range(heads)]
    gain_rows.append(jnp.zeros((16 - heads, HEAD_DIM), f32))
    gain_all[me] = jnp.concatenate(gain_rows, axis=0).astype(bf16)
    hid_all[me] = hid[...]
    pl.semaphore_wait(barrier, ntp - 1 + ncb - 1)

    buffers, phases = [hid_all, gain_all], [NORM, GAIN]
    direct, passed = share(buffers, phases)
    relayed = []
    total = jnp.zeros((rows, 1), f32)

    size = rows * heads
    place = lax.broadcasted_iota(jnp.int32, (size, size), 0)
    column = lax.broadcasted_iota(jnp.int32, (size, size), 1)
    source = ((place // per_dev) % heads) * rows + (place // blk) * per_dev + place % per_dev
    perm = (column == source).astype(f32).astype(bf16)
    arriving = []
    for n, origin in enumerate(visits):
        if n == 1:
            for copy in passed:
                copy.wait_recv()
        elif 2 <= n < 1 + chips:
            relayed.append([])
            for b, p, copy in zip(buffers, phases, direct[n - 2]):
                copy.wait_recv()
                relayed[-1].append(
                    put(b.at[origin], b.at[origin], p, chips + far[n - 2], "tp", twin)
                )
        elif n >= 1 + chips:
            for copy in relayed[n - 1 - chips]:
                copy.wait_recv()
        piece = hid_all[origin].astype(f32)
        gains = gain_all[origin].astype(f32)
        total = total + jnp.sum(piece * piece, axis=1, keepdims=True)
        scaled = jnp.concatenate(
            [
                piece[:, h * HEAD_DIM : (h + 1) * HEAD_DIM] * gains[h : h + 1, :]
                for h in range(heads)
            ],
            axis=1,
        ).astype(bf16)
        weights["q", n].wait()
        if n == 4:
            load("e", embed, ve, ntp)
            load("k", keys, vk, ntp + 1)
            load("v", values, vv, ntp + 2)
        if n == 6:
            load("o", w_out, vo, ntp + 3)
            load("i", w_in, vi, ntp + 4)
            load("g", w_gu, vg, ntp + 5)
            load("d", w_down, vd, ntp + 6)
        inv = lax.rsqrt(total / D + eps)
        for i in range(3):
            term = jnp.dot(scaled, vq[i, part_of(origin), :], preferred_element_type=f32)
            if n:
                term = term + acc[i]
            if n < ntp - 1:
                acc[i] = term
                continue
            full = (term * inv).astype(bf16)
            stacked = jnp.concatenate(
                [full[:, h * HEAD_DIM : (h + 1) * HEAD_DIM] for h in range(heads)], axis=0
            )
            moved = jnp.dot(perm, stacked, preferred_element_type=f32).astype(bf16)
            qkv_send[i] = moved.reshape(ntp, blk, HEAD_DIM)
            arriving += [
                put(qkv_send.at[i, tp_at(j)], qkv_recv.at[i, me], QKV + i, j, "tp", tp_at(j))
                for j in order
            ]
            qkv_recv[i, me] = qkv_send[i, me]

    weights["e"].wait()
    codes = lax.broadcasted_iota(jnp.int32, (tokens.shape[1], CARD), 1)
    for local in range(steps):
        spread = jnp.broadcast_to(tokens[local : local + 1, :], (128, tokens.shape[1]))
        chosen = jnp.transpose(spread)[:, 0:1]
        one_hot = (chosen == codes).astype(f32).astype(bf16)
        emb[local] = jnp.dot(one_hot, ve[local], preferred_element_type=f32).astype(bf16)
    carry = put(emb.at[steps - 1], carried, CARRY, 1, "cb", cb_at(1))
    weights["k"].wait()
    weights["v"].wait()
    for copy in arriving:
        copy.wait_recv()

    scale = 1.0 / math.sqrt(HEAD_DIM)
    slots = per_dev * CACHE
    row = lax.broadcasted_iota(jnp.int32, (blk, slots), 0)
    col = lax.broadcasted_iota(jnp.int32, (blk, slots), 1)
    count = jnp.zeros((blk, slots), jnp.int32)
    for r in range(per_dev):
        count = jnp.where(col // CACHE == r, lengths[r], count)
    live = (row % per_dev == col // CACHE) & (col % CACHE < count)
    head_of = lax.broadcasted_iota(jnp.int32, (blk, HEAD_DIM), 0) // per_dev
    queries, products = [], []
    for s in range(ntp):
        query = qkv_recv[0, s].astype(f32)
        spread = jnp.concatenate(
            [jnp.where(head_of == h, query, 0.0) for h in range(heads)], axis=1
        ).astype(bf16)
        cols = slice(s * feat, (s + 1) * feat)
        old_keys = vk[:, :, cols].reshape(slots, feat)
        products.append(
            lax.dot_general(
                old_keys, spread, (((1,), (1,)), ((), ())), preferred_element_type=f32
            )
        )
        queries.append(query)
    products = jnp.transpose(jnp.concatenate(products, axis=1))
    for s in range(ntp):
        query = queries[s]
        key_new = qkv_recv[1, s].astype(f32)
        value_new = qkv_recv[2, s].astype(f32)
        cols = slice(s * feat, (s + 1) * feat)
        scores = products[s * blk : (s + 1) * blk, :] * scale
        scores = jnp.where(live, scores, -1e30)
        fresh = jnp.sum(query * key_new, axis=1, keepdims=True) * scale
        top = jnp.maximum(jnp.max(scores, axis=1, keepdims=True), fresh)
        weight = jnp.exp(scores - top)
        weight_new = jnp.exp(fresh - top)
        norm = jnp.sum(weight, axis=1, keepdims=True) + weight_new
        probs = (weight / norm).astype(bf16)
        prob_new = (weight_new / norm).astype(bf16).astype(f32)
        old_values = vv[:, :, cols].reshape(slots, feat)
        wide = jnp.dot(probs, old_values, preferred_element_type=f32)
        mixed = prob_new * value_new
        for h in range(heads):
            mixed = mixed + jnp.where(
                head_of == h, wide[:, h * HEAD_DIM : (h + 1) * HEAD_DIM], 0.0
            )
        att_send[s] = mixed.astype(bf16)
    arriving = [
        put(att_send.at[tp_at(i)], att_recv.at[me], BACK, i, "tp", tp_at(i)) for i in order
    ]
    att_recv[me] = att_send[me]
    for copy in arriving:
        copy.wait_recv()
    gathered = att_recv[...].reshape(ntp * blk, HEAD_DIM)
    place = lax.broadcasted_iota(jnp.int32, (rows, ntp * blk), 0)
    column = lax.broadcasted_iota(jnp.int32, (rows, ntp * blk), 1)
    for h in range(heads):
        source = (place // per_dev) * blk + h * per_dev + place % per_dev
        pick = (column == source).astype(f32).astype(bf16)
        returned[:, h * HEAD_DIM : (h + 1) * HEAD_DIM] = jnp.dot(
            pick, gathered, preferred_element_type=f32
        ).astype(bf16)

    weights["o"].wait()

    def projected(device):
        cols = pl.ds(pl.multiple_of(device * feat, feat), feat)
        return jnp.dot(returned[...], vo[:, cols], preferred_element_type=f32)

    for z in range(chips):
        o_twin[0, z] = projected(2 * z + 1 - core).astype(bf16)
    merged = put(o_twin.at[0], o_twin.at[1], OUT, 0, "tp", twin)
    mine = [projected(same_core(j)) for j in far + [0]]
    merged.wait_recv()
    arriving = []
    for j, term in zip(far, mine):
        o_send[j] = (term + o_twin[1, lax.rem(chip + j, chips)].astype(f32)).astype(bf16)
        arriving.append(put(o_send.at[j], o_recv.at[j], OUT, j, "tp", same_core(j)))
    attn = mine[-1] + o_twin[1, chip].astype(f32)
    for j, copy in zip(far, arriving):
        copy.wait_recv()
        attn = attn + o_recv[j].astype(f32)
    temporal = (hid[...].astype(f32) + attn).astype(bf16)
    out_t[...] = temporal
    frame[grp] = temporal

    arriving = [
        put(frame.at[grp], frame.at[grp], FRAME, i, "cb", cb_at(i)) for i in range(1, ncb)
    ]
    weights["i"].wait()
    carry.wait_recv()
    for copy in arriving:
        copy.wait_recv()
    lhs = frame[...].reshape(ncb * rows, feat)

    own_cols = pl.ds(pl.multiple_of(me * dfeat, dfeat), dfeat)

    def rows_of(device):
        return pl.ds(pl.multiple_of(device * drows, drows), drows)

    def cols_of(device):
        return pl.ds(pl.multiple_of(device * dfeat, dfeat), dfeat)

    merged = []
    for local in range(steps):
        part[local] = jnp.dot(lhs, vi[local], preferred_element_type=f32)
        before = carried[...] if local == 0 else emb[local - 1]
        part[local, :, own_cols] = part[local, :, own_cols] + before.astype(f32)
        for z in range(chips):
            x_twin[local, 0, z] = part[local, rows_of(2 * z + 1 - core), :].astype(bf16)
        merged.append(
            put(x_twin.at[local, 0], x_twin.at[local, 1], XSUM + local, 0, "tp", twin)
        )
    arriving = []
    for local in range(steps):
        merged[local].wait_recv()
        copies = []
        for j in far:
            x_send[local, j] = (
                part[local, rows_of(same_core(j)), :]
                + x_twin[local, 1, lax.rem(chip + j, chips)].astype(f32)
            ).astype(bf16)
            copies.append(
                put(x_send.at[local, j], x_recv.at[local, j], XSUM + local, j, "tp", same_core(j))
            )
        arriving.append(copies)
    gathers = []
    for local in range(steps):
        x = part[local, rows_of(me), :] + x_twin[local, 1, chip].astype(f32)
        for j, copy in zip(far, arriving[local]):
            copy.wait_recv()
            x = x + x_recv[local, j].astype(f32)
        x_own[local] = x
        inv = lax.rsqrt(jnp.sum(x * x, axis=1, keepdims=True) / DD + eps)
        gains = depth_gain[local : local + 1, :].astype(f32)
        xn_all[local, me] = (x * inv * gains).astype(bf16)
        gathers.append(share([xn_all.at[local]], [XN + local]))

    weights["g"].wait()
    weights["d"].wait()
    contract_last = (((1,), (1,)), ((), ()))
    gathers[0] = pass_on([xn_all.at[0]], [XN], gathers[0])
    merged, summed = [], []

    def send_down(local):
        merged[local].wait_recv()
        copies = []
        for j in far:
            d_send[local, j] = (
                part[local, :, cols_of(same_core(j))]
                + d_twin[local, 1, lax.rem(chip + j, chips)].astype(f32)
            ).astype(bf16)
            copies.append(
                put(d_send.at[local, j], d_recv.at[local, j], DOWN + local, j, "tp", same_core(j))
            )
        summed.append(copies)

    for local in range(steps):
        for copy in gathers[local]:
            copy.wait_recv()
        lhs = xn_all[local].reshape(ntp * drows, DD)
        gate = lax.dot_general(lhs, vg[local, 0], contract_last, preferred_element_type=f32)
        upper = lax.dot_general(lhs, vg[local, 1], contract_last, preferred_element_type=f32)
        act = (jax.nn.silu(gate) * upper).astype(bf16)
        if local + 1 < steps:
            gathers[local + 1] = pass_on(
                [xn_all.at[local + 1]], [XN + local + 1], gathers[local + 1]
            )
        part[local] = jnp.dot(act, vd[local], preferred_element_type=f32)
        part[local, rows_of(me), :] = part[local, rows_of(me), :] + x_own[local]
        for z in range(chips):
            d_twin[local, 0, z] = part[local, :, cols_of(2 * z + 1 - core)].astype(bf16)
        merged.append(
            put(d_twin.at[local, 0], d_twin.at[local, 1], DOWN + local, 0, "tp", twin)
        )
        if local:
            send_down(local - 1)
    send_down(steps - 1)
    for local in range(steps):
        y = part[local, :, own_cols] + d_twin[local, 1, chip].astype(f32)
        for j, copy in zip(far, summed[local]):
            copy.wait_recv()
            y = y + d_recv[local, j].astype(f32)
        out_d[local] = y.astype(out_d.dtype)
    for copy in sent:
        copy.wait_send()


def finish(temporal, depth, out_t, out_d):
    out_t[...] = temporal[...]
    out_d[...] = depth[...]


def fits(mesh, hidden_in, w_in):
    ntp, ncb = mesh.shape["tp"], mesh.shape["cb"]
    rows, feat = hidden_in.shape[0] // ncb, hidden_in.shape[1] // ntp
    steps = w_in.shape[0] // ncb
    return (
        steps == 2
        and ntp % 2 == 0
        and rows * ncb == 128
        and ntp == 8
        and feat % HEAD_DIM == 0
        and feat // HEAD_DIM <= 16
        and rows % ntp == 0
        and (rows // ntp * (feat // HEAD_DIM)) % 16 == 0
        and (rows * ncb) % (16 * ntp) == 0
        and (DD // ntp) % 128 == 0
    )


def fused(
    hidden_in,
    norm_gain,
    w_qkv,
    w_out,
    cache_keys,
    cache_values,
    lengths,
    tokens,
    w_in,
    embed,
    depth_gain,
    w_gate_up,
    w_down,
):
    ntp, ncb = lax.axis_size("tp"), lax.axis_size("cb")
    f32, bf16 = jnp.float32, jnp.bfloat16
    rows, feat = hidden_in.shape
    blk = rows // ntp * (feat // HEAD_DIM)
    steps = w_in.shape[0]
    chips = ntp // 2
    total_rows = rows * ncb
    drows, dfeat = total_rows // ntp, DD // ntp
    vmem = pl.BlockSpec(memory_space=pltpu.VMEM)
    hbm = pl.BlockSpec(memory_space=pl.ANY)
    big = [w_qkv, w_out, cache_keys, cache_values, w_in, embed, jnp.swapaxes(w_gate_up, 2, 3), w_down]
    scratch = [pltpu.VMEM(a.shape, a.dtype) for a in big] + [
        pltpu.VMEM((ntp, rows, feat), bf16),
        pltpu.VMEM((ntp, 16, HEAD_DIM), bf16),
        pltpu.VMEM((3, rows, feat), f32),
        pltpu.VMEM((3, ntp, blk, HEAD_DIM), bf16),
        pltpu.VMEM((3, ntp, blk, HEAD_DIM), bf16),
        pltpu.VMEM((ntp, blk, HEAD_DIM), bf16),
        pltpu.VMEM((ntp, blk, HEAD_DIM), bf16),
        pltpu.VMEM((rows, feat), bf16),
        pltpu.VMEM((2, chips, rows, feat), bf16),
        pltpu.VMEM((chips, rows, feat), bf16),
        pltpu.VMEM((chips, rows, feat), bf16),
        pltpu.VMEM((ncb, rows, feat), bf16),
        pltpu.VMEM((steps, total_rows, dfeat), bf16),
        pltpu.VMEM((total_rows, dfeat), bf16),
        pltpu.VMEM((steps, total_rows, DD), f32),
        pltpu.VMEM((steps, 2, chips, drows, DD), bf16),
        pltpu.VMEM((steps, chips, drows, DD), bf16),
        pltpu.VMEM((steps, chips, drows, DD), bf16),
        pltpu.VMEM((steps, drows, DD), f32),
        pltpu.VMEM((steps, ntp, drows, DD), bf16),
        pltpu.VMEM((steps, 2, chips, total_rows, dfeat), bf16),
        pltpu.VMEM((steps, chips, total_rows, dfeat), bf16),
        pltpu.VMEM((steps, chips, total_rows, dfeat), bf16),
        pltpu.SemaphoreType.DMA((ntp + 7,)),
        pltpu.SemaphoreType.DMA((PHASES, ntp)),
        pltpu.SemaphoreType.DMA((PHASES, ntp)),
    ]
    temporal, depth = pl.pallas_call(
        functools.partial(frame_kernel, ntp, ncb),
        out_shape=(
            jax.ShapeDtypeStruct((rows, feat), bf16),
            jax.ShapeDtypeStruct((steps, total_rows, dfeat), bf16),
        ),
        in_specs=[vmem, vmem, pl.BlockSpec(memory_space=pltpu.SMEM), vmem, vmem] + [hbm] * 8,
        out_specs=(vmem, vmem),
        scratch_shapes=scratch,
        compiler_params=pltpu.CompilerParams(
            collective_id=0, has_side_effects=True, vmem_limit_bytes=60 * 1024 * 1024
        ),
    )(
        hidden_in,
        norm_gain,
        lengths,
        tokens.T,
        depth_gain,
        *big,
    )
    return pl.pallas_call(
        finish,
        out_shape=(
            jax.ShapeDtypeStruct(temporal.shape, bf16),
            jax.ShapeDtypeStruct(depth.shape, bf16),
        ),
        in_specs=[vmem, vmem],
        out_specs=(vmem, vmem),
    )(temporal, depth)


def solution(mesh):
    in_specs = (
        P("cb", "tp"),
        P("tp"),
        P(None, None, "tp"),
        P("tp", None),
        P(("cb", "tp"), None, None),
        P(("cb", "tp"), None, None),
        P(("cb", "tp")),
        P(None, "cb"),
        P("cb", "tp", None),
        P("cb", None, "tp"),
        P("cb", None),
        P("cb", None, None, "tp"),
        P("cb", "tp", None),
    )
    out_specs = (P("cb", "tp"), P("cb", None, "tp"))

    def run(*args):
        body = fused if fits(mesh, args[0], args[8]) else per_device
        return jax.shard_map(
            body, mesh=mesh, in_specs=in_specs, out_specs=out_specs, check_vma=False
        )(*args)

    return run
```

```python
import functools
import math

import jax
import jax.numpy as jnp
from jax import lax
from jax.experimental import pallas as pl
from jax.experimental.pallas import tpu as pltpu
from jax.sharding import PartitionSpec as P

D = 4096
HEADS = 32
HEAD_DIM = 128
DD = 1024
CARD = 2048
CACHE = 64


eps = 1e-05


def from_behind(value, axis, steps):
    count = lax.axis_size(axis)
    pairs = [(source, (source + steps) % count) for source in range(count)]
    return lax.ppermute(value, axis, pairs)


def per_device(
    hidden_in,
    norm_gain,
    w_qkv,
    w_out,
    cache_keys,
    cache_values,
    lengths,
    tokens,
    w_in,
    embed,
    depth_gain,
    w_gate_up,
    w_down,
):
    width_tp = lax.axis_size("tp")
    group_rows, feat_loc = hidden_in.shape
    hid32 = hidden_in.astype(jnp.float32)
    sum_sq = lax.psum(jnp.sum(hid32 * hid32, axis=1), "tp")
    normed = (hid32 * lax.rsqrt(sum_sq / D + eps)[:, None] * norm_gain.astype(jnp.float32)).astype(
        jnp.bfloat16
    )
    qkv = jnp.einsum(
        "rd,idf->rif",
        lax.all_gather(normed, "tp", axis=1, tiled=True),
        w_qkv,
        preferred_element_type=jnp.float32,
    ).astype(jnp.bfloat16)
    per_dev = group_rows // width_tp
    arrived = lax.all_to_all(
        qkv.reshape(width_tp, per_dev, 3, feat_loc), "tp", split_axis=0, concat_axis=3, tiled=True
    )
    arrived = arrived.reshape(per_dev, 3, D)
    scale = 1.0 / math.sqrt(HEAD_DIM)
    query_h = arrived[:, 0].reshape(per_dev, HEADS, HEAD_DIM)
    key_new = arrived[:, 1].reshape(per_dev, HEADS, HEAD_DIM)
    value_new = arrived[:, 2].reshape(per_dev, HEADS, HEAD_DIM)
    keys_h = cache_keys.reshape(per_dev, CACHE, HEADS, HEAD_DIM)
    values_h = cache_values.reshape(per_dev, CACHE, HEADS, HEAD_DIM)
    scores = (
        jnp.einsum("rhe,rphe->rhp", query_h, keys_h, preferred_element_type=jnp.float32) * scale
    )
    live = lax.broadcasted_iota(jnp.int32, (1, 1, CACHE), 2) < lengths[:, None, None]
    scores = jnp.where(live, scores, -1e30)
    fresh = jnp.sum(query_h.astype(jnp.float32) * key_new.astype(jnp.float32), axis=-1) * scale
    top = jnp.maximum(jnp.max(scores, axis=-1), fresh)
    weights = jnp.exp(scores - top[..., None])
    weight_new = jnp.exp(fresh - top)
    total = jnp.sum(weights, axis=-1) + weight_new
    probs = (weights / total[..., None]).astype(jnp.bfloat16)
    prob_new = (weight_new / total).astype(jnp.bfloat16)
    mixed = jnp.einsum("rhp,rphe->rhe", probs, values_h, preferred_element_type=jnp.float32)
    mixed = mixed + prob_new.astype(jnp.float32)[..., None] * value_new.astype(jnp.float32)
    attended = mixed.reshape(per_dev, width_tp, feat_loc).astype(jnp.bfloat16)
    returned = lax.all_to_all(attended, "tp", split_axis=1, concat_axis=0, tiled=True).reshape(
        group_rows, feat_loc
    )
    partial_value = jnp.dot(returned, w_out, preferred_element_type=jnp.float32)
    attn_sum = lax.psum_scatter(partial_value, "tp", scatter_dimension=1, tiled=True)
    temporal_out = (hid32 + attn_sum).astype(jnp.bfloat16)
    frame = lax.all_gather(temporal_out, "cb", axis=0, tiled=True)
    steps_here = w_in.shape[0]
    depth_loc = embed.shape[2]
    column_start = lax.axis_index("tp") * depth_loc
    codes = lax.broadcasted_iota(jnp.int32, (1, CARD), 1)
    embedded = []
    for local in range(steps_here):
        one_hot = (tokens[:, local][:, None] == codes).astype(jnp.bfloat16)
        embedded.append(
            jnp.dot(one_hot, embed[local], preferred_element_type=jnp.float32).astype(jnp.bfloat16)
        )
    carried = from_behind(embedded[steps_here - 1], "cb", 1)
    previous = [carried] + embedded[: steps_here - 1]
    results = []
    for local in range(steps_here):
        term = jnp.dot(frame, w_in[local], preferred_element_type=jnp.float32)
        gain_all = depth_gain[local].astype(jnp.float32)
        x_loc = lax.psum_scatter(term, "tp", scatter_dimension=1, tiled=True) + previous[
            local
        ].astype(jnp.float32)
        sum_d = lax.psum(jnp.sum(x_loc * x_loc, axis=1), "tp")
        gain_loc = lax.dynamic_slice_in_dim(gain_all, column_start, depth_loc, 0)
        xn_loc = (x_loc * lax.rsqrt(sum_d / DD + eps)[:, None] * gain_loc).astype(jnp.bfloat16)
        weights_step = w_gate_up[local]
        gate_up = jnp.einsum(
            "rd,idf->irf",
            lax.all_gather(xn_loc, "tp", axis=1, tiled=True),
            weights_step,
            preferred_element_type=jnp.float32,
        )
        act = (jax.nn.silu(gate_up[0]) * gate_up[1]).astype(jnp.bfloat16)
        down_term = jnp.dot(act, w_down[local], preferred_element_type=jnp.float32)
        down_sum = lax.psum_scatter(down_term, "tp", scatter_dimension=1, tiled=True)
        results.append((x_loc + down_sum).astype(jnp.bfloat16))
    return (temporal_out, jnp.stack(results))


MESH = pl.DeviceIdType.MESH
NORM, GAIN, CARRY, BACK, OUT, FRAME, XSUM, XN, DOWN, QKV = 0, 1, 2, 3, 4, 5, 6, 8, 10, 12
PHASES = 15


def frame_kernel(
    ntp,
    ncb,
    hid,
    gain,
    lengths,
    tokens,
    depth_gain,
    w_qkv,
    w_out,
    keys,
    values,
    w_in,
    embed,
    w_gu,
    w_down,
    out_t,
    out_d,
    vq,
    vo,
    vk,
    vv,
    vi,
    ve,
    vg,
    vd,
    hid_all,
    gain_all,
    acc,
    qkv_send,
    qkv_recv,
    att_send,
    att_recv,
    returned,
    o_twin,
    o_send,
    o_recv,
    frame,
    emb,
    carried,
    part,
    x_twin,
    x_send,
    x_recv,
    x_own,
    xn_all,
    d_twin,
    d_send,
    d_recv,
    wsem,
    ssem,
    rsem,
):
    f32, bf16 = jnp.float32, jnp.bfloat16
    me = lax.axis_index("tp")
    grp = lax.axis_index("cb")
    rows, feat = hid.shape
    per_dev = rows // ntp
    heads = feat // HEAD_DIM
    blk = per_dev * heads
    steps = w_in.shape[0]
    drows = frame.shape[0] * rows // ntp
    dfeat = DD // ntp
    order = sorted(range(1, ntp), key=lambda i: abs(i - ntp // 2))
    chips = ntp // 2
    core = lax.rem(me, 2)
    chip = lax.div(me, 2)
    twin = chip * 2 + 1 - core
    far = sorted(range(1, chips), key=lambda j: abs(j - chips // 2))

    weights = {}

    def load(name, source, target, index):
        copy = pltpu.make_async_copy(source, target, wsem.at[index])
        copy.start()
        weights[name] = copy


    sent = []

    def put(source, target, phase, i, axis, device):
        copy = pltpu.make_async_remote_copy(
            src_ref=source,
            dst_ref=target,
            send_sem=ssem.at[phase, i],
            recv_sem=rsem.at[phase, i],
            device_id={axis: device},
            device_id_type=MESH,
        )
        copy.start()
        sent.append(copy)
        return copy

    def tp_at(i):
        return lax.rem(me + i, ntp)

    def cb_at(i):
        return lax.rem(grp + i, ncb)

    def same_core(j):
        return lax.rem(chip + j, chips) * 2 + core

    def share(buffers, phases):
        direct = [
            [put(b.at[me], b.at[me], p, j, "tp", same_core(j)) for b, p in zip(buffers, phases)]
            for j in far
        ]
        passed = [put(b.at[me], b.at[me], p, chips, "tp", twin) for b, p in zip(buffers, phases)]
        return direct, passed

    def pass_on(buffers, phases, state):
        direct, passed = state
        for j, copies in zip(far, direct):
            origin = same_core(chips - j)
            for b, p, copy in zip(buffers, phases, copies):
                copy.wait_recv()
                passed.append(put(b.at[origin], b.at[origin], p, chips + j, "tp", twin))
        return passed

    barrier = pltpu.get_barrier_semaphore()
    for i in range(1, ntp):
        pl.semaphore_signal(barrier, inc=1, device_id={"tp": tp_at(i)}, device_id_type=MESH)
    for i in range(1, ncb):
        pl.semaphore_signal(barrier, inc=1, device_id={"cb": cb_at(i)}, device_id_type=MESH)

    def part_of(device):
        return pl.ds(pl.multiple_of(device * feat, feat), feat)

    visits = [me, twin]
    visits += [same_core(chips - j) for j in far]
    visits += [same_core(chips - j) + 1 - 2 * core for j in far]
    for n, origin in enumerate(visits):
        load(
            ("q", n), w_qkv.at[:, part_of(origin), :], vq.at[:, part_of(origin), :], n
        )
    gain32 = gain[...].reshape(1, feat).astype(f32)
    gain_rows = [gain32[:, h * HEAD_DIM : (h + 1) * HEAD_DIM] for h in range(heads)]
    gain_rows.append(jnp.zeros((16 - heads, HEAD_DIM), f32))
    gain_all[me] = jnp.concatenate(gain_rows, axis=0).astype(bf16)
    hid_all[me] = hid[...]
    pl.semaphore_wait(barrier, ntp - 1 + ncb - 1)

    buffers, phases = [hid_all, gain_all], [NORM, GAIN]
    direct, passed = share(buffers, phases)
    relayed = []
    total = jnp.zeros((rows, 1), f32)

    size = rows * heads
    place = lax.broadcasted_iota(jnp.int32, (size, size), 0)
    column = lax.broadcasted_iota(jnp.int32, (size, size), 1)
    source = ((place // per_dev) % heads) * rows + (place // blk) * per_dev + place % per_dev
    perm = (column == source).astype(f32).astype(bf16)
    arriving = []
    for n, origin in enumerate(visits):
        if n == 1:
            for copy in passed:
                copy.wait_recv()
        elif 2 <= n < 1 + chips:
            relayed.append([])
            for b, p, copy in zip(buffers, phases, direct[n - 2]):
                copy.wait_recv()
                relayed[-1].append(
                    put(b.at[origin], b.at[origin], p, chips + far[n - 2], "tp", twin)
                )
        elif n >= 1 + chips:
            for copy in relayed[n - 1 - chips]:
                copy.wait_recv()
        piece = hid_all[origin].astype(f32)
        gains = gain_all[origin].astype(f32)
        total = total + jnp.sum(piece * piece, axis=1, keepdims=True)
        scaled = jnp.concatenate(
            [
                piece[:, h * HEAD_DIM : (h + 1) * HEAD_DIM] * gains[h : h + 1, :]
                for h in range(heads)
            ],
            axis=1,
        ).astype(bf16)
        weights["q", n].wait()
        if n == 4:
            load("e", embed, ve, ntp)
            load("k", keys, vk, ntp + 1)
            load("v", values, vv, ntp + 2)
        if n == 6:
            load("o", w_out, vo, ntp + 3)
            load("i", w_in, vi, ntp + 4)
            load("g", w_gu, vg, ntp + 5)
            load("d", w_down, vd, ntp + 6)
        inv = lax.rsqrt(total / D + eps)
        for i in range(3):
            term = jnp.dot(scaled, vq[i, part_of(origin), :], preferred_element_type=f32)
            if n:
                term = term + acc[i]
            if n < ntp - 1:
                acc[i] = term
                continue
            full = (term * inv).astype(bf16)
            stacked = jnp.concatenate(
                [full[:, h * HEAD_DIM : (h + 1) * HEAD_DIM] for h in range(heads)], axis=0
            )
            moved = jnp.dot(perm, stacked, preferred_element_type=f32).astype(bf16)
            qkv_send[i] = moved.reshape(ntp, blk, HEAD_DIM)
            arriving += [
                put(qkv_send.at[i, tp_at(j)], qkv_recv.at[i, me], QKV + i, j, "tp", tp_at(j))
                for j in order
            ]
            qkv_recv[i, me] = qkv_send[i, me]

    weights["e"].wait()
    codes = lax.broadcasted_iota(jnp.int32, (tokens.shape[1], CARD), 1)
    for local in range(steps):
        spread = jnp.broadcast_to(tokens[local : local + 1, :], (128, tokens.shape[1]))
        chosen = jnp.transpose(spread)[:, 0:1]
        one_hot = (chosen == codes).astype(f32).astype(bf16)
        emb[local] = jnp.dot(one_hot, ve[local], preferred_element_type=f32).astype(bf16)
    carry = put(emb.at[steps - 1], carried, CARRY, 1, "cb", cb_at(1))
    weights["k"].wait()
    weights["v"].wait()
    for copy in arriving:
        copy.wait_recv()

    scale = 1.0 / math.sqrt(HEAD_DIM)
    slots = per_dev * CACHE
    row = lax.broadcasted_iota(jnp.int32, (blk, slots), 0)
    col = lax.broadcasted_iota(jnp.int32, (blk, slots), 1)
    count = jnp.zeros((blk, slots), jnp.int32)
    for r in range(per_dev):
        count = jnp.where(col // CACHE == r, lengths[r], count)
    live = (row % per_dev == col // CACHE) & (col % CACHE < count)
    head_of = lax.broadcasted_iota(jnp.int32, (blk, HEAD_DIM), 0) // per_dev
    queries, products = [], []
    for s in range(ntp):
        query = qkv_recv[0, s].astype(f32)
        spread = jnp.concatenate(
            [jnp.where(head_of == h, query, 0.0) for h in range(heads)], axis=1
        ).astype(bf16)
        cols = slice(s * feat, (s + 1) * feat)
        old_keys = vk[:, :, cols].reshape(slots, feat)
        products.append(
            lax.dot_general(
                old_keys, spread, (((1,), (1,)), ((), ())), preferred_element_type=f32
            )
        )
        queries.append(query)
    products = jnp.transpose(jnp.concatenate(products, axis=1))
    for s in range(ntp):
        query = queries[s]
        key_new = qkv_recv[1, s].astype(f32)
        value_new = qkv_recv[2, s].astype(f32)
        cols = slice(s * feat, (s + 1) * feat)
        scores = products[s * blk : (s + 1) * blk, :] * scale
        scores = jnp.where(live, scores, -1e30)
        fresh = jnp.sum(query * key_new, axis=1, keepdims=True) * scale
        top = jnp.maximum(jnp.max(scores, axis=1, keepdims=True), fresh)
        weight = jnp.exp(scores - top)
        weight_new = jnp.exp(fresh - top)
        norm = jnp.sum(weight, axis=1, keepdims=True) + weight_new
        probs = (weight / norm).astype(bf16)
        prob_new = (weight_new / norm).astype(bf16).astype(f32)
        old_values = vv[:, :, cols].reshape(slots, feat)
        wide = jnp.dot(probs, old_values, preferred_element_type=f32)
        mixed = prob_new * value_new
        for h in range(heads):
            mixed = mixed + jnp.where(
                head_of == h, wide[:, h * HEAD_DIM : (h + 1) * HEAD_DIM], 0.0
            )
        att_send[s] = mixed.astype(bf16)
    arriving = [
        put(att_send.at[tp_at(i)], att_recv.at[me], BACK, i, "tp", tp_at(i)) for i in order
    ]
    att_recv[me] = att_send[me]
    for copy in arriving:
        copy.wait_recv()
    gathered = att_recv[...].reshape(ntp * blk, HEAD_DIM)
    place = lax.broadcasted_iota(jnp.int32, (rows, ntp * blk), 0)
    column = lax.broadcasted_iota(jnp.int32, (rows, ntp * blk), 1)
    for h in range(heads):
        source = (place // per_dev) * blk + h * per_dev + place % per_dev
        pick = (column == source).astype(f32).astype(bf16)
        returned[:, h * HEAD_DIM : (h + 1) * HEAD_DIM] = jnp.dot(
            pick, gathered, preferred_element_type=f32
        ).astype(bf16)

    weights["o"].wait()

    def projected(device):
        cols = pl.ds(pl.multiple_of(device * feat, feat), feat)
        return jnp.dot(returned[...], vo[:, cols], preferred_element_type=f32)

    for z in range(chips):
        o_twin[0, z] = projected(2 * z + 1 - core).astype(bf16)
    merged = put(o_twin.at[0], o_twin.at[1], OUT, 0, "tp", twin)
    mine = [projected(same_core(j)) for j in far + [0]]
    merged.wait_recv()
    arriving = []
    for j, term in zip(far, mine):
        o_send[j] = (term + o_twin[1, lax.rem(chip + j, chips)].astype(f32)).astype(bf16)
        arriving.append(put(o_send.at[j], o_recv.at[j], OUT, j, "tp", same_core(j)))
    attn = mine[-1] + o_twin[1, chip].astype(f32)
    for j, copy in zip(far, arriving):
        copy.wait_recv()
        attn = attn + o_recv[j].astype(f32)
    temporal = (hid[...].astype(f32) + attn).astype(bf16)
    out_t[...] = temporal
    frame[grp] = temporal

    arriving = [
        put(frame.at[grp], frame.at[grp], FRAME, i, "cb", cb_at(i)) for i in range(1, ncb)
    ]
    weights["i"].wait()
    carry.wait_recv()
    for copy in arriving:
        copy.wait_recv()
    lhs = frame[...].reshape(ncb * rows, feat)

    own_cols = pl.ds(pl.multiple_of(me * dfeat, dfeat), dfeat)

    def rows_of(device):
        return pl.ds(pl.multiple_of(device * drows, drows), drows)

    def cols_of(device):
        return pl.ds(pl.multiple_of(device * dfeat, dfeat), dfeat)

    merged = []
    for local in range(steps):
        part[local] = jnp.dot(lhs, vi[local], preferred_element_type=f32)
        before = carried[...] if local == 0 else emb[local - 1]
        part[local, :, own_cols] = part[local, :, own_cols] + before.astype(f32)
        for z in range(chips):
            x_twin[local, 0, z] = part[local, rows_of(2 * z + 1 - core), :].astype(bf16)
        merged.append(
            put(x_twin.at[local, 0], x_twin.at[local, 1], XSUM + local, 0, "tp", twin)
        )
    arriving = []
    for local in range(steps):
        merged[local].wait_recv()
        copies = []
        for j in far:
            x_send[local, j] = (
                part[local, rows_of(same_core(j)), :]
                + x_twin[local, 1, lax.rem(chip + j, chips)].astype(f32)
            ).astype(bf16)
            copies.append(
                put(x_send.at[local, j], x_recv.at[local, j], XSUM + local, j, "tp", same_core(j))
            )
        arriving.append(copies)
    gathers = []
    for local in range(steps):
        x = part[local, rows_of(me), :] + x_twin[local, 1, chip].astype(f32)
        for j, copy in zip(far, arriving[local]):
            copy.wait_recv()
            x = x + x_recv[local, j].astype(f32)
        x_own[local] = x
        inv = lax.rsqrt(jnp.sum(x * x, axis=1, keepdims=True) / DD + eps)
        gains = depth_gain[local : local + 1, :].astype(f32)
        xn_all[local, me] = (x * inv * gains).astype(bf16)
        gathers.append(share([xn_all.at[local]], [XN + local]))

    weights["g"].wait()
    weights["d"].wait()
    contract_last = (((1,), (1,)), ((), ()))
    gathers[0] = pass_on([xn_all.at[0]], [XN], gathers[0])
    merged, summed = [], []

    def send_down(local):
        merged[local].wait_recv()
        copies = []
        for j in far:
            d_send[local, j] = (
                part[local, :, cols_of(same_core(j))]
                + d_twin[local, 1, lax.rem(chip + j, chips)].astype(f32)
            ).astype(bf16)
            copies.append(
                put(d_send.at[local, j], d_recv.at[local, j], DOWN + local, j, "tp", same_core(j))
            )
        summed.append(copies)

    for local in range(steps):
        for copy in gathers[local]:
            copy.wait_recv()
        lhs = xn_all[local].reshape(ntp * drows, DD)
        gate = lax.dot_general(vg[local, 0], lhs, contract_last, preferred_element_type=f32)
        upper = lax.dot_general(vg[local, 1], lhs, contract_last, preferred_element_type=f32)
        act = jnp.transpose(jax.nn.silu(gate) * upper).astype(bf16)
        if local + 1 < steps:
            gathers[local + 1] = pass_on(
                [xn_all.at[local + 1]], [XN + local + 1], gathers[local + 1]
            )
        if local:
            send_down(local - 1)
        part[local] = jnp.dot(act, vd[local], preferred_element_type=f32)
        part[local, rows_of(me), :] = part[local, rows_of(me), :] + x_own[local]
        for z in range(chips):
            d_twin[local, 0, z] = part[local, :, cols_of(2 * z + 1 - core)].astype(bf16)
        merged.append(
            put(d_twin.at[local, 0], d_twin.at[local, 1], DOWN + local, 0, "tp", twin)
        )
    send_down(steps - 1)
    for local in range(steps):
        y = part[local, :, own_cols] + d_twin[local, 1, chip].astype(f32)
        for j, copy in zip(far, summed[local]):
            copy.wait_recv()
            y = y + d_recv[local, j].astype(f32)
        out_d[local] = y.astype(out_d.dtype)
    for copy in sent:
        copy.wait_send()


def finish(temporal, depth, out_t, out_d):
    out_t[...] = temporal[...]
    out_d[...] = depth[...]


def fits(mesh, hidden_in, w_in):
    ntp, ncb = mesh.shape["tp"], mesh.shape["cb"]
    rows, feat = hidden_in.shape[0] // ncb, hidden_in.shape[1] // ntp
    steps = w_in.shape[0] // ncb
    return (
        steps == 2
        and ntp % 2 == 0
        and rows * ncb == 128
        and ntp == 8
        and feat % HEAD_DIM == 0
        and feat // HEAD_DIM <= 16
        and rows % ntp == 0
        and (rows // ntp * (feat // HEAD_DIM)) % 16 == 0
        and (rows * ncb) % (16 * ntp) == 0
        and (DD // ntp) % 128 == 0
    )


def fused(
    hidden_in,
    norm_gain,
    w_qkv,
    w_out,
    cache_keys,
    cache_values,
    lengths,
    tokens,
    w_in,
    embed,
    depth_gain,
    w_gate_up,
    w_down,
):
    ntp, ncb = lax.axis_size("tp"), lax.axis_size("cb")
    f32, bf16 = jnp.float32, jnp.bfloat16
    rows, feat = hidden_in.shape
    blk = rows // ntp * (feat // HEAD_DIM)
    steps = w_in.shape[0]
    chips = ntp // 2
    total_rows = rows * ncb
    drows, dfeat = total_rows // ntp, DD // ntp
    vmem = pl.BlockSpec(memory_space=pltpu.VMEM)
    hbm = pl.BlockSpec(memory_space=pl.ANY)
    big = [w_qkv, w_out, cache_keys, cache_values, w_in, embed, jnp.swapaxes(w_gate_up, 2, 3), w_down]
    scratch = [pltpu.VMEM(a.shape, a.dtype) for a in big] + [
        pltpu.VMEM((ntp, rows, feat), bf16),
        pltpu.VMEM((ntp, 16, HEAD_DIM), bf16),
        pltpu.VMEM((3, rows, feat), f32),
        pltpu.VMEM((3, ntp, blk, HEAD_DIM), bf16),
        pltpu.VMEM((3, ntp, blk, HEAD_DIM), bf16),
        pltpu.VMEM((ntp, blk, HEAD_DIM), bf16),
        pltpu.VMEM((ntp, blk, HEAD_DIM), bf16),
        pltpu.VMEM((rows, feat), bf16),
        pltpu.VMEM((2, chips, rows, feat), bf16),
        pltpu.VMEM((chips, rows, feat), bf16),
        pltpu.VMEM((chips, rows, feat), bf16),
        pltpu.VMEM((ncb, rows, feat), bf16),
        pltpu.VMEM((steps, total_rows, dfeat), bf16),
        pltpu.VMEM((total_rows, dfeat), bf16),
        pltpu.VMEM((steps, total_rows, DD), f32),
        pltpu.VMEM((steps, 2, chips, drows, DD), bf16),
        pltpu.VMEM((steps, chips, drows, DD), bf16),
        pltpu.VMEM((steps, chips, drows, DD), bf16),
        pltpu.VMEM((steps, drows, DD), f32),
        pltpu.VMEM((steps, ntp, drows, DD), bf16),
        pltpu.VMEM((steps, 2, chips, total_rows, dfeat), bf16),
        pltpu.VMEM((steps, chips, total_rows, dfeat), bf16),
        pltpu.VMEM((steps, chips, total_rows, dfeat), bf16),
        pltpu.SemaphoreType.DMA((ntp + 7,)),
        pltpu.SemaphoreType.DMA((PHASES, ntp)),
        pltpu.SemaphoreType.DMA((PHASES, ntp)),
    ]
    temporal, depth = pl.pallas_call(
        functools.partial(frame_kernel, ntp, ncb),
        out_shape=(
            jax.ShapeDtypeStruct((rows, feat), bf16),
            jax.ShapeDtypeStruct((steps, total_rows, dfeat), bf16),
        ),
        in_specs=[vmem, vmem, pl.BlockSpec(memory_space=pltpu.SMEM), vmem, vmem] + [hbm] * 8,
        out_specs=(vmem, vmem),
        scratch_shapes=scratch,
        compiler_params=pltpu.CompilerParams(
            collective_id=0, has_side_effects=True, vmem_limit_bytes=60 * 1024 * 1024
        ),
    )(
        hidden_in,
        norm_gain,
        lengths,
        tokens.T,
        depth_gain,
        *big,
    )
    return pl.pallas_call(
        finish,
        out_shape=(
            jax.ShapeDtypeStruct(temporal.shape, bf16),
            jax.ShapeDtypeStruct(depth.shape, bf16),
        ),
        in_specs=[vmem, vmem],
        out_specs=(vmem, vmem),
    )(temporal, depth)


def solution(mesh):
    in_specs = (
        P("cb", "tp"),
        P("tp"),
        P(None, None, "tp"),
        P("tp", None),
        P(("cb", "tp"), None, None),
        P(("cb", "tp"), None, None),
        P(("cb", "tp")),
        P(None, "cb"),
        P("cb", "tp", None),
        P("cb", None, "tp"),
        P("cb", None),
        P("cb", None, None, "tp"),
        P("cb", "tp", None),
    )
    out_specs = (P("cb", "tp"), P("cb", None, "tp"))

    def run(*args):
        body = fused if fits(mesh, args[0], args[8]) else per_device
        return jax.shard_map(
            body, mesh=mesh, in_specs=in_specs, out_specs=out_specs, check_vma=False
        )(*args)

    return run
```

```python
import functools
import math

import jax
import jax.numpy as jnp
from jax import lax
from jax.experimental import pallas as pl
from jax.experimental.pallas import tpu as pltpu
from jax.sharding import PartitionSpec as P

D = 4096
HEADS = 32
HEAD_DIM = 128
DD = 1024
CARD = 2048
CACHE = 64


eps = 1e-05


def from_behind(value, axis, steps):
    count = lax.axis_size(axis)
    pairs = [(source, (source + steps) % count) for source in range(count)]
    return lax.ppermute(value, axis, pairs)


def per_device(
    hidden_in,
    norm_gain,
    w_qkv,
    w_out,
    cache_keys,
    cache_values,
    lengths,
    tokens,
    w_in,
    embed,
    depth_gain,
    w_gate_up,
    w_down,
):
    width_tp = lax.axis_size("tp")
    group_rows, feat_loc = hidden_in.shape
    hid32 = hidden_in.astype(jnp.float32)
    sum_sq = lax.psum(jnp.sum(hid32 * hid32, axis=1), "tp")
    normed = (hid32 * lax.rsqrt(sum_sq / D + eps)[:, None] * norm_gain.astype(jnp.float32)).astype(
        jnp.bfloat16
    )
    qkv = jnp.einsum(
        "rd,idf->rif",
        lax.all_gather(normed, "tp", axis=1, tiled=True),
        w_qkv,
        preferred_element_type=jnp.float32,
    ).astype(jnp.bfloat16)
    per_dev = group_rows // width_tp
    arrived = lax.all_to_all(
        qkv.reshape(width_tp, per_dev, 3, feat_loc), "tp", split_axis=0, concat_axis=3, tiled=True
    )
    arrived = arrived.reshape(per_dev, 3, D)
    scale = 1.0 / math.sqrt(HEAD_DIM)
    query_h = arrived[:, 0].reshape(per_dev, HEADS, HEAD_DIM)
    key_new = arrived[:, 1].reshape(per_dev, HEADS, HEAD_DIM)
    value_new = arrived[:, 2].reshape(per_dev, HEADS, HEAD_DIM)
    keys_h = cache_keys.reshape(per_dev, CACHE, HEADS, HEAD_DIM)
    values_h = cache_values.reshape(per_dev, CACHE, HEADS, HEAD_DIM)
    scores = (
        jnp.einsum("rhe,rphe->rhp", query_h, keys_h, preferred_element_type=jnp.float32) * scale
    )
    live = lax.broadcasted_iota(jnp.int32, (1, 1, CACHE), 2) < lengths[:, None, None]
    scores = jnp.where(live, scores, -1e30)
    fresh = jnp.sum(query_h.astype(jnp.float32) * key_new.astype(jnp.float32), axis=-1) * scale
    top = jnp.maximum(jnp.max(scores, axis=-1), fresh)
    weights = jnp.exp(scores - top[..., None])
    weight_new = jnp.exp(fresh - top)
    total = jnp.sum(weights, axis=-1) + weight_new
    probs = (weights / total[..., None]).astype(jnp.bfloat16)
    prob_new = (weight_new / total).astype(jnp.bfloat16)
    mixed = jnp.einsum("rhp,rphe->rhe", probs, values_h, preferred_element_type=jnp.float32)
    mixed = mixed + prob_new.astype(jnp.float32)[..., None] * value_new.astype(jnp.float32)
    attended = mixed.reshape(per_dev, width_tp, feat_loc).astype(jnp.bfloat16)
    returned = lax.all_to_all(attended, "tp", split_axis=1, concat_axis=0, tiled=True).reshape(
        group_rows, feat_loc
    )
    partial_value = jnp.dot(returned, w_out, preferred_element_type=jnp.float32)
    attn_sum = lax.psum_scatter(partial_value, "tp", scatter_dimension=1, tiled=True)
    temporal_out = (hid32 + attn_sum).astype(jnp.bfloat16)
    frame = lax.all_gather(temporal_out, "cb", axis=0, tiled=True)
    steps_here = w_in.shape[0]
    depth_loc = embed.shape[2]
    column_start = lax.axis_index("tp") * depth_loc
    codes = lax.broadcasted_iota(jnp.int32, (1, CARD), 1)
    embedded = []
    for local in range(steps_here):
        one_hot = (tokens[:, local][:, None] == codes).astype(jnp.bfloat16)
        embedded.append(
            jnp.dot(one_hot, embed[local], preferred_element_type=jnp.float32).astype(jnp.bfloat16)
        )
    carried = from_behind(embedded[steps_here - 1], "cb", 1)
    previous = [carried] + embedded[: steps_here - 1]
    results = []
    for local in range(steps_here):
        term = jnp.dot(frame, w_in[local], preferred_element_type=jnp.float32)
        gain_all = depth_gain[local].astype(jnp.float32)
        x_loc = lax.psum_scatter(term, "tp", scatter_dimension=1, tiled=True) + previous[
            local
        ].astype(jnp.float32)
        sum_d = lax.psum(jnp.sum(x_loc * x_loc, axis=1), "tp")
        gain_loc = lax.dynamic_slice_in_dim(gain_all, column_start, depth_loc, 0)
        xn_loc = (x_loc * lax.rsqrt(sum_d / DD + eps)[:, None] * gain_loc).astype(jnp.bfloat16)
        weights_step = w_gate_up[local]
        gate_up = jnp.einsum(
            "rd,idf->irf",
            lax.all_gather(xn_loc, "tp", axis=1, tiled=True),
            weights_step,
            preferred_element_type=jnp.float32,
        )
        act = (jax.nn.silu(gate_up[0]) * gate_up[1]).astype(jnp.bfloat16)
        down_term = jnp.dot(act, w_down[local], preferred_element_type=jnp.float32)
        down_sum = lax.psum_scatter(down_term, "tp", scatter_dimension=1, tiled=True)
        results.append((x_loc + down_sum).astype(jnp.bfloat16))
    return (temporal_out, jnp.stack(results))


MESH = pl.DeviceIdType.MESH
NORM, GAIN, CARRY, BACK, OUT, FRAME, XSUM, XN, DOWN, QKV = 0, 1, 2, 3, 4, 5, 6, 8, 10, 12
PHASES = 13


def frame_kernel(
    ntp,
    ncb,
    hid,
    gain,
    lengths,
    tokens,
    depth_gain,
    w_qkv,
    w_out,
    keys,
    values,
    w_in,
    embed,
    w_gu,
    w_down,
    out_t,
    out_d,
    vq,
    vo,
    vk,
    vv,
    vi,
    ve,
    vg,
    vd,
    hid_all,
    gain_all,
    acc,
    qkv_send,
    qkv_recv,
    att_send,
    att_recv,
    returned,
    o_twin,
    o_send,
    o_recv,
    frame,
    emb,
    carried,
    part,
    x_twin,
    x_send,
    x_recv,
    x_own,
    xn_all,
    d_twin,
    d_send,
    d_recv,
    wsem,
    ssem,
    rsem,
):
    f32, bf16 = jnp.float32, jnp.bfloat16
    me = lax.axis_index("tp")
    grp = lax.axis_index("cb")
    rows, feat = hid.shape
    per_dev = rows // ntp
    heads = feat // HEAD_DIM
    blk = per_dev * heads
    steps = w_in.shape[0]
    drows = frame.shape[0] * rows // ntp
    dfeat = DD // ntp
    order = sorted(range(1, ntp), key=lambda i: abs(i - ntp // 2))
    chips = ntp // 2
    core = lax.rem(me, 2)
    chip = lax.div(me, 2)
    twin = chip * 2 + 1 - core
    far = sorted(range(1, chips), key=lambda j: abs(j - chips // 2))

    weights = {}

    def load(name, source, target, index):
        copy = pltpu.make_async_copy(source, target, wsem.at[index])
        copy.start()
        weights[name] = copy


    sent = []

    def put(source, target, phase, i, axis, device):
        copy = pltpu.make_async_remote_copy(
            src_ref=source,
            dst_ref=target,
            send_sem=ssem.at[phase, i],
            recv_sem=rsem.at[phase, i],
            device_id={axis: device},
            device_id_type=MESH,
        )
        copy.start()
        sent.append(copy)
        return copy

    def tp_at(i):
        return lax.rem(me + i, ntp)

    def cb_at(i):
        return lax.rem(grp + i, ncb)

    def same_core(j):
        return lax.rem(chip + j, chips) * 2 + core

    def share(buffers, phases):
        direct = [
            [put(b.at[me], b.at[me], p, j, "tp", same_core(j)) for b, p in zip(buffers, phases)]
            for j in far
        ]
        passed = [put(b.at[me], b.at[me], p, chips, "tp", twin) for b, p in zip(buffers, phases)]
        return direct, passed

    def pass_on(buffers, phases, state):
        direct, passed = state
        for j, copies in zip(far, direct):
            origin = same_core(chips - j)
            for b, p, copy in zip(buffers, phases, copies):
                copy.wait_recv()
                passed.append(put(b.at[origin], b.at[origin], p, chips + j, "tp", twin))
        return passed

    barrier = pltpu.get_barrier_semaphore()
    for i in range(1, ntp):
        pl.semaphore_signal(barrier, inc=1, device_id={"tp": tp_at(i)}, device_id_type=MESH)
    for i in range(1, ncb):
        pl.semaphore_signal(barrier, inc=1, device_id={"cb": cb_at(i)}, device_id_type=MESH)

    def part_of(device):
        return pl.ds(pl.multiple_of(device * feat, feat), feat)

    visits = [me, twin]
    visits += [same_core(chips - j) for j in far]
    visits += [same_core(chips - j) + 1 - 2 * core for j in far]
    for n, origin in enumerate(visits):
        load(
            ("q", n), w_qkv.at[:, part_of(origin), :], vq.at[:, part_of(origin), :], n
        )
    gain32 = gain[...].reshape(1, feat).astype(f32)
    gain_rows = [gain32[:, h * HEAD_DIM : (h + 1) * HEAD_DIM] for h in range(heads)]
    gain_rows.append(jnp.zeros((16 - heads, HEAD_DIM), f32))
    gain_all[me] = jnp.concatenate(gain_rows, axis=0).astype(bf16)
    hid_all[me] = hid[...]
    pl.semaphore_wait(barrier, ntp - 1 + ncb - 1)

    buffers, phases = [hid_all, gain_all], [NORM, GAIN]
    direct, passed = share(buffers, phases)
    relayed = []
    total = jnp.zeros((rows, 1), f32)

    size = rows * heads
    place = lax.broadcasted_iota(jnp.int32, (size, size), 0)
    column = lax.broadcasted_iota(jnp.int32, (size, size), 1)
    source = ((place // per_dev) % heads) * rows + (place // blk) * per_dev + place % per_dev
    perm = (column == source).astype(f32).astype(bf16)
    for n, origin in enumerate(visits):
        if n == 1:
            for copy in passed:
                copy.wait_recv()
        elif 2 <= n < 1 + chips:
            relayed.append([])
            for b, p, copy in zip(buffers, phases, direct[n - 2]):
                copy.wait_recv()
                relayed[-1].append(
                    put(b.at[origin], b.at[origin], p, chips + far[n - 2], "tp", twin)
                )
        elif n >= 1 + chips:
            for copy in relayed[n - 1 - chips]:
                copy.wait_recv()
        piece = hid_all[origin].astype(f32)
        gains = gain_all[origin].astype(f32)
        total = total + jnp.sum(piece * piece, axis=1, keepdims=True)
        scaled = jnp.concatenate(
            [
                piece[:, h * HEAD_DIM : (h + 1) * HEAD_DIM] * gains[h : h + 1, :]
                for h in range(heads)
            ],
            axis=1,
        ).astype(bf16)
        weights["q", n].wait()
        if n == 4:
            load("e", embed, ve, ntp)
            load("k", keys, vk, ntp + 1)
            load("v", values, vv, ntp + 2)
        if n == 6:
            load("o", w_out, vo, ntp + 3)
            load("i", w_in, vi, ntp + 4)
            load("g", w_gu, vg, ntp + 5)
            load("d", w_down, vd, ntp + 6)
        inv = lax.rsqrt(total / D + eps)
        for i in range(3):
            term = jnp.dot(scaled, vq[i, part_of(origin), :], preferred_element_type=f32)
            if n:
                term = term + acc[i]
            if n < ntp - 1:
                acc[i] = term
                continue
            full = (term * inv).astype(bf16)
            stacked = jnp.concatenate(
                [full[:, h * HEAD_DIM : (h + 1) * HEAD_DIM] for h in range(heads)], axis=0
            )
            moved = jnp.dot(perm, stacked, preferred_element_type=f32).astype(bf16)
            qkv_send[i] = moved.reshape(ntp, blk, HEAD_DIM)
    arriving = [
        put(qkv_send.at[:, tp_at(j)], qkv_recv.at[:, me], QKV, j, "tp", tp_at(j)) for j in order
    ]
    qkv_recv[:, me] = qkv_send[:, me]

    weights["e"].wait()
    codes = lax.broadcasted_iota(jnp.int32, (tokens.shape[1], CARD), 1)

    def embed_tokens(local):
        spread = jnp.broadcast_to(tokens[local : local + 1, :], (128, tokens.shape[1]))
        chosen = jnp.transpose(spread)[:, 0:1]
        one_hot = (chosen == codes).astype(f32).astype(bf16)
        emb[local] = jnp.dot(one_hot, ve[local], preferred_element_type=f32).astype(bf16)

    embed_tokens(steps - 1)
    carry = put(emb.at[steps - 1], carried, CARRY, 1, "cb", cb_at(1))
    weights["k"].wait()
    weights["v"].wait()
    for copy in arriving:
        copy.wait_recv()

    scale = 1.0 / math.sqrt(HEAD_DIM)
    slots = per_dev * CACHE
    row = lax.broadcasted_iota(jnp.int32, (blk, slots), 0)
    col = lax.broadcasted_iota(jnp.int32, (blk, slots), 1)
    count = jnp.zeros((blk, slots), jnp.int32)
    for r in range(per_dev):
        count = jnp.where(col // CACHE == r, lengths[r], count)
    live = (row % per_dev == col // CACHE) & (col % CACHE < count)
    head_of = lax.broadcasted_iota(jnp.int32, (blk, HEAD_DIM), 0) // per_dev
    queries, products = [], []
    for s in range(ntp):
        query = qkv_recv[0, s].astype(f32)
        spread = jnp.concatenate(
            [jnp.where(head_of == h, query, 0.0) for h in range(heads)], axis=1
        ).astype(bf16)
        cols = slice(s * feat, (s + 1) * feat)
        old_keys = vk[:, :, cols].reshape(slots, feat)
        products.append(
            lax.dot_general(
                old_keys, spread, (((1,), (1,)), ((), ())), preferred_element_type=f32
            )
        )
        queries.append(query)
    products = jnp.transpose(jnp.concatenate(products, axis=1))
    for s in range(ntp):
        query = queries[s]
        key_new = qkv_recv[1, s].astype(f32)
        value_new = qkv_recv[2, s].astype(f32)
        cols = slice(s * feat, (s + 1) * feat)
        scores = products[s * blk : (s + 1) * blk, :] * scale
        scores = jnp.where(live, scores, -1e30)
        fresh = jnp.sum(query * key_new, axis=1, keepdims=True) * scale
        top = jnp.maximum(jnp.max(scores, axis=1, keepdims=True), fresh)
        weight = jnp.exp(scores - top)
        weight_new = jnp.exp(fresh - top)
        norm = jnp.sum(weight, axis=1, keepdims=True) + weight_new
        probs = (weight / norm).astype(bf16)
        prob_new = (weight_new / norm).astype(bf16).astype(f32)
        old_values = vv[:, :, cols].reshape(slots, feat)
        wide = jnp.dot(probs, old_values, preferred_element_type=f32)
        mixed = prob_new * value_new
        for h in range(heads):
            mixed = mixed + jnp.where(
                head_of == h, wide[:, h * HEAD_DIM : (h + 1) * HEAD_DIM], 0.0
            )
        att_send[s] = mixed.astype(bf16)
    arriving = [
        put(att_send.at[tp_at(i)], att_recv.at[me], BACK, i, "tp", tp_at(i)) for i in order
    ]
    att_recv[me] = att_send[me]
    for copy in arriving:
        copy.wait_recv()
    gathered = att_recv[...].reshape(ntp * blk, HEAD_DIM)
    place = lax.broadcasted_iota(jnp.int32, (rows, ntp * blk), 0)
    column = lax.broadcasted_iota(jnp.int32, (rows, ntp * blk), 1)
    for h in range(heads):
        source = (place // per_dev) * blk + h * per_dev + place % per_dev
        pick = (column == source).astype(f32).astype(bf16)
        returned[:, h * HEAD_DIM : (h + 1) * HEAD_DIM] = jnp.dot(
            pick, gathered, preferred_element_type=f32
        ).astype(bf16)

    weights["o"].wait()

    def projected(device):
        cols = pl.ds(pl.multiple_of(device * feat, feat), feat)
        return jnp.dot(returned[...], vo[:, cols], preferred_element_type=f32)

    for z in range(chips):
        o_twin[0, z] = projected(2 * z + 1 - core).astype(bf16)
    merged = put(o_twin.at[0], o_twin.at[1], OUT, 0, "tp", twin)
    mine = [projected(same_core(j)) for j in far + [0]]
    merged.wait_recv()
    arriving = []
    for j, term in zip(far, mine):
        o_send[j] = (term + o_twin[1, lax.rem(chip + j, chips)].astype(f32)).astype(bf16)
        arriving.append(put(o_send.at[j], o_recv.at[j], OUT, j, "tp", same_core(j)))
    attn = mine[-1] + o_twin[1, chip].astype(f32)
    for j, copy in zip(far, arriving):
        copy.wait_recv()
        attn = attn + o_recv[j].astype(f32)
    temporal = (hid[...].astype(f32) + attn).astype(bf16)
    out_t[...] = temporal
    frame[grp] = temporal

    arriving = [
        put(frame.at[grp], frame.at[grp], FRAME, i, "cb", cb_at(i)) for i in range(1, ncb)
    ]
    for local in range(steps - 1):
        embed_tokens(local)
    weights["i"].wait()
    carry.wait_recv()
    for copy in arriving:
        copy.wait_recv()
    lhs = frame[...].reshape(ncb * rows, feat)

    own_cols = pl.ds(pl.multiple_of(me * dfeat, dfeat), dfeat)

    def rows_of(device):
        return pl.ds(pl.multiple_of(device * drows, drows), drows)

    def cols_of(device):
        return pl.ds(pl.multiple_of(device * dfeat, dfeat), dfeat)

    merged, arriving = [], []

    def send_input(local):
        merged[local].wait_recv()
        copies = []
        for j in far:
            x_send[local, j] = (
                part[local, rows_of(same_core(j)), :]
                + x_twin[local, 1, lax.rem(chip + j, chips)].astype(f32)
            ).astype(bf16)
            copies.append(
                put(x_send.at[local, j], x_recv.at[local, j], XSUM + local, j, "tp", same_core(j))
            )
        arriving.append(copies)

    for local in range(steps):
        part[local] = jnp.dot(lhs, vi[local], preferred_element_type=f32)
        before = carried[...] if local == 0 else emb[local - 1]
        part[local, :, own_cols] = part[local, :, own_cols] + before.astype(f32)
        if local:
            send_input(local - 1)
        for z in range(chips):
            x_twin[local, 0, z] = part[local, rows_of(2 * z + 1 - core), :].astype(bf16)
        merged.append(
            put(x_twin.at[local, 0], x_twin.at[local, 1], XSUM + local, 0, "tp", twin)
        )
    send_input(steps - 1)
    gathers = []
    for local in range(steps):
        x = part[local, rows_of(me), :] + x_twin[local, 1, chip].astype(f32)
        for j, copy in zip(far, arriving[local]):
            copy.wait_recv()
            x = x + x_recv[local, j].astype(f32)
        x_own[local] = x
        inv = lax.rsqrt(jnp.sum(x * x, axis=1, keepdims=True) / DD + eps)
        gains = depth_gain[local : local + 1, :].astype(f32)
        xn_all[local, me] = (x * inv * gains).astype(bf16)
        gathers.append(share([xn_all.at[local]], [XN + local]))

    weights["g"].wait()
    weights["d"].wait()
    contract_last = (((1,), (1,)), ((), ()))
    gathers[0] = pass_on([xn_all.at[0]], [XN], gathers[0])
    merged, summed = [], []

    def send_down(local):
        merged[local].wait_recv()
        copies = []
        for j in far:
            d_send[local, j] = (
                part[local, :, cols_of(same_core(j))]
                + d_twin[local, 1, lax.rem(chip + j, chips)].astype(f32)
            ).astype(bf16)
            copies.append(
                put(d_send.at[local, j], d_recv.at[local, j], DOWN + local, j, "tp", same_core(j))
            )
        summed.append(copies)

    for local in range(steps):
        for copy in gathers[local]:
            copy.wait_recv()
        lhs = xn_all[local].reshape(ntp * drows, DD)
        gate = lax.dot_general(vg[local, 0], lhs, contract_last, preferred_element_type=f32)
        upper = lax.dot_general(vg[local, 1], lhs, contract_last, preferred_element_type=f32)
        act = jnp.transpose(jax.nn.silu(gate) * upper).astype(bf16)
        if local + 1 < steps:
            gathers[local + 1] = pass_on(
                [xn_all.at[local + 1]], [XN + local + 1], gathers[local + 1]
            )
        if local:
            send_down(local - 1)
        part[local] = jnp.dot(act, vd[local], preferred_element_type=f32)
        part[local, rows_of(me), :] = part[local, rows_of(me), :] + x_own[local]
        for z in range(chips):
            d_twin[local, 0, z] = part[local, :, cols_of(2 * z + 1 - core)].astype(bf16)
        merged.append(
            put(d_twin.at[local, 0], d_twin.at[local, 1], DOWN + local, 0, "tp", twin)
        )
    send_down(steps - 1)
    early = len(sent) - len(far) * steps
    for copy in sent[:early]:
        copy.wait_send()
    for local in range(steps):
        y = part[local, :, own_cols] + d_twin[local, 1, chip].astype(f32)
        for j, copy in zip(far, summed[local]):
            copy.wait_recv()
            y = y + d_recv[local, j].astype(f32)
        out_d[local] = y.astype(out_d.dtype)
    for copy in sent[early:]:
        copy.wait_send()


def finish(temporal, depth, out_t, out_d):
    out_t[...] = temporal[...]
    out_d[...] = depth[...]


def fits(mesh, hidden_in, w_in):
    ntp, ncb = mesh.shape["tp"], mesh.shape["cb"]
    rows, feat = hidden_in.shape[0] // ncb, hidden_in.shape[1] // ntp
    steps = w_in.shape[0] // ncb
    return (
        steps == 2
        and ntp % 2 == 0
        and rows * ncb == 128
        and ntp == 8
        and feat % HEAD_DIM == 0
        and feat // HEAD_DIM <= 16
        and rows % ntp == 0
        and (rows // ntp * (feat // HEAD_DIM)) % 16 == 0
        and (rows * ncb) % (16 * ntp) == 0
        and (DD // ntp) % 128 == 0
    )


def fused(
    hidden_in,
    norm_gain,
    w_qkv,
    w_out,
    cache_keys,
    cache_values,
    lengths,
    tokens,
    w_in,
    embed,
    depth_gain,
    w_gate_up,
    w_down,
):
    ntp, ncb = lax.axis_size("tp"), lax.axis_size("cb")
    f32, bf16 = jnp.float32, jnp.bfloat16
    rows, feat = hidden_in.shape
    blk = rows // ntp * (feat // HEAD_DIM)
    steps = w_in.shape[0]
    chips = ntp // 2
    total_rows = rows * ncb
    drows, dfeat = total_rows // ntp, DD // ntp
    vmem = pl.BlockSpec(memory_space=pltpu.VMEM)
    hbm = pl.BlockSpec(memory_space=pl.ANY)
    big = [w_qkv, w_out, cache_keys, cache_values, w_in, embed, jnp.swapaxes(w_gate_up, 2, 3), w_down]
    scratch = [pltpu.VMEM(a.shape, a.dtype) for a in big] + [
        pltpu.VMEM((ntp, rows, feat), bf16),
        pltpu.VMEM((ntp, 16, HEAD_DIM), bf16),
        pltpu.VMEM((3, rows, feat), f32),
        pltpu.VMEM((3, ntp, blk, HEAD_DIM), bf16),
        pltpu.VMEM((3, ntp, blk, HEAD_DIM), bf16),
        pltpu.VMEM((ntp, blk, HEAD_DIM), bf16),
        pltpu.VMEM((ntp, blk, HEAD_DIM), bf16),
        pltpu.VMEM((rows, feat), bf16),
        pltpu.VMEM((2, chips, rows, feat), bf16),
        pltpu.VMEM((chips, rows, feat), bf16),
        pltpu.VMEM((chips, rows, feat), bf16),
        pltpu.VMEM((ncb, rows, feat), bf16),
        pltpu.VMEM((steps, total_rows, dfeat), bf16),
        pltpu.VMEM((total_rows, dfeat), bf16),
        pltpu.VMEM((steps, total_rows, DD), f32),
        pltpu.VMEM((steps, 2, chips, drows, DD), bf16),
        pltpu.VMEM((steps, chips, drows, DD), bf16),
        pltpu.VMEM((steps, chips, drows, DD), bf16),
        pltpu.VMEM((steps, drows, DD), f32),
        pltpu.VMEM((steps, ntp, drows, DD), bf16),
        pltpu.VMEM((steps, 2, chips, total_rows, dfeat), bf16),
        pltpu.VMEM((steps, chips, total_rows, dfeat), bf16),
        pltpu.VMEM((steps, chips, total_rows, dfeat), bf16),
        pltpu.SemaphoreType.DMA((ntp + 7,)),
        pltpu.SemaphoreType.DMA((PHASES, ntp)),
        pltpu.SemaphoreType.DMA((PHASES, ntp)),
    ]
    temporal, depth = pl.pallas_call(
        functools.partial(frame_kernel, ntp, ncb),
        out_shape=(
            jax.ShapeDtypeStruct((rows, feat), bf16),
            jax.ShapeDtypeStruct((steps, total_rows, dfeat), bf16),
        ),
        in_specs=[vmem, vmem, pl.BlockSpec(memory_space=pltpu.SMEM), vmem, vmem] + [hbm] * 8,
        out_specs=(vmem, vmem),
        scratch_shapes=scratch,
        compiler_params=pltpu.CompilerParams(
            collective_id=0, has_side_effects=True, vmem_limit_bytes=60 * 1024 * 1024
        ),
    )(
        hidden_in,
        norm_gain,
        lengths,
        tokens.T,
        depth_gain,
        *big,
    )
    return pl.pallas_call(
        finish,
        out_shape=(
            jax.ShapeDtypeStruct(temporal.shape, bf16),
            jax.ShapeDtypeStruct(depth.shape, bf16),
        ),
        in_specs=[vmem, vmem],
        out_specs=(vmem, vmem),
    )(temporal, depth)


def solution(mesh):
    in_specs = (
        P("cb", "tp"),
        P("tp"),
        P(None, None, "tp"),
        P("tp", None),
        P(("cb", "tp"), None, None),
        P(("cb", "tp"), None, None),
        P(("cb", "tp")),
        P(None, "cb"),
        P("cb", "tp", None),
        P("cb", None, "tp"),
        P("cb", None),
        P("cb", None, None, "tp"),
        P("cb", "tp", None),
    )
    out_specs = (P("cb", "tp"), P("cb", None, "tp"))

    def run(*args):
        body = fused if fits(mesh, args[0], args[8]) else per_device
        return jax.shard_map(
            body, mesh=mesh, in_specs=in_specs, out_specs=out_specs, check_vma=False
        )(*args)

    return run
```

```python
import functools
import math

import jax
import jax.numpy as jnp
from jax import lax
from jax.experimental import pallas as pl
from jax.experimental.pallas import tpu as pltpu
from jax.sharding import PartitionSpec as P

D = 4096
HEADS = 32
HEAD_DIM = 128
DD = 1024
CARD = 2048
CACHE = 64


eps = 1e-05


def from_behind(value, axis, steps):
    count = lax.axis_size(axis)
    pairs = [(source, (source + steps) % count) for source in range(count)]
    return lax.ppermute(value, axis, pairs)


def per_device(
    hidden_in,
    norm_gain,
    w_qkv,
    w_out,
    cache_keys,
    cache_values,
    lengths,
    tokens,
    w_in,
    embed,
    depth_gain,
    w_gate_up,
    w_down,
):
    width_tp = lax.axis_size("tp")
    group_rows, feat_loc = hidden_in.shape
    hid32 = hidden_in.astype(jnp.float32)
    sum_sq = lax.psum(jnp.sum(hid32 * hid32, axis=1), "tp")
    normed = (hid32 * lax.rsqrt(sum_sq / D + eps)[:, None] * norm_gain.astype(jnp.float32)).astype(
        jnp.bfloat16
    )
    qkv = jnp.einsum(
        "rd,idf->rif",
        lax.all_gather(normed, "tp", axis=1, tiled=True),
        w_qkv,
        preferred_element_type=jnp.float32,
    ).astype(jnp.bfloat16)
    per_dev = group_rows // width_tp
    arrived = lax.all_to_all(
        qkv.reshape(width_tp, per_dev, 3, feat_loc), "tp", split_axis=0, concat_axis=3, tiled=True
    )
    arrived = arrived.reshape(per_dev, 3, D)
    scale = 1.0 / math.sqrt(HEAD_DIM)
    query_h = arrived[:, 0].reshape(per_dev, HEADS, HEAD_DIM)
    key_new = arrived[:, 1].reshape(per_dev, HEADS, HEAD_DIM)
    value_new = arrived[:, 2].reshape(per_dev, HEADS, HEAD_DIM)
    keys_h = cache_keys.reshape(per_dev, CACHE, HEADS, HEAD_DIM)
    values_h = cache_values.reshape(per_dev, CACHE, HEADS, HEAD_DIM)
    scores = (
        jnp.einsum("rhe,rphe->rhp", query_h, keys_h, preferred_element_type=jnp.float32) * scale
    )
    live = lax.broadcasted_iota(jnp.int32, (1, 1, CACHE), 2) < lengths[:, None, None]
    scores = jnp.where(live, scores, -1e30)
    fresh = jnp.sum(query_h.astype(jnp.float32) * key_new.astype(jnp.float32), axis=-1) * scale
    top = jnp.maximum(jnp.max(scores, axis=-1), fresh)
    weights = jnp.exp(scores - top[..., None])
    weight_new = jnp.exp(fresh - top)
    total = jnp.sum(weights, axis=-1) + weight_new
    probs = (weights / total[..., None]).astype(jnp.bfloat16)
    prob_new = (weight_new / total).astype(jnp.bfloat16)
    mixed = jnp.einsum("rhp,rphe->rhe", probs, values_h, preferred_element_type=jnp.float32)
    mixed = mixed + prob_new.astype(jnp.float32)[..., None] * value_new.astype(jnp.float32)
    attended = mixed.reshape(per_dev, width_tp, feat_loc).astype(jnp.bfloat16)
    returned = lax.all_to_all(attended, "tp", split_axis=1, concat_axis=0, tiled=True).reshape(
        group_rows, feat_loc
    )
    partial_value = jnp.dot(returned, w_out, preferred_element_type=jnp.float32)
    attn_sum = lax.psum_scatter(partial_value, "tp", scatter_dimension=1, tiled=True)
    temporal_out = (hid32 + attn_sum).astype(jnp.bfloat16)
    frame = lax.all_gather(temporal_out, "cb", axis=0, tiled=True)
    steps_here = w_in.shape[0]
    depth_loc = embed.shape[2]
    column_start = lax.axis_index("tp") * depth_loc
    codes = lax.broadcasted_iota(jnp.int32, (1, CARD), 1)
    embedded = []
    for local in range(steps_here):
        one_hot = (tokens[:, local][:, None] == codes).astype(jnp.bfloat16)
        embedded.append(
            jnp.dot(one_hot, embed[local], preferred_element_type=jnp.float32).astype(jnp.bfloat16)
        )
    carried = from_behind(embedded[steps_here - 1], "cb", 1)
    previous = [carried] + embedded[: steps_here - 1]
    results = []
    for local in range(steps_here):
        term = jnp.dot(frame, w_in[local], preferred_element_type=jnp.float32)
        gain_all = depth_gain[local].astype(jnp.float32)
        x_loc = lax.psum_scatter(term, "tp", scatter_dimension=1, tiled=True) + previous[
            local
        ].astype(jnp.float32)
        sum_d = lax.psum(jnp.sum(x_loc * x_loc, axis=1), "tp")
        gain_loc = lax.dynamic_slice_in_dim(gain_all, column_start, depth_loc, 0)
        xn_loc = (x_loc * lax.rsqrt(sum_d / DD + eps)[:, None] * gain_loc).astype(jnp.bfloat16)
        weights_step = w_gate_up[local]
        gate_up = jnp.einsum(
            "rd,idf->irf",
            lax.all_gather(xn_loc, "tp", axis=1, tiled=True),
            weights_step,
            preferred_element_type=jnp.float32,
        )
        act = (jax.nn.silu(gate_up[0]) * gate_up[1]).astype(jnp.bfloat16)
        down_term = jnp.dot(act, w_down[local], preferred_element_type=jnp.float32)
        down_sum = lax.psum_scatter(down_term, "tp", scatter_dimension=1, tiled=True)
        results.append((x_loc + down_sum).astype(jnp.bfloat16))
    return (temporal_out, jnp.stack(results))


MESH = pl.DeviceIdType.MESH
NORM, GAIN, CARRY, BACK, OUT, FRAME, XSUM, XN, DOWN, QKV = 0, 1, 2, 3, 4, 5, 6, 8, 10, 12
PHASES = 13


def frame_kernel(
    ntp,
    ncb,
    hid,
    gain,
    lengths,
    tokens,
    depth_gain,
    w_qkv,
    w_out,
    keys,
    values,
    w_in,
    embed,
    w_gu,
    w_down,
    out_t,
    out_d,
    vq,
    vo,
    vk,
    vv,
    vi,
    ve,
    vg,
    vd,
    hid_all,
    gain_all,
    acc,
    qkv_send,
    qkv_recv,
    att_send,
    att_recv,
    returned,
    o_twin,
    o_send,
    o_recv,
    frame,
    emb,
    carried,
    part,
    x_twin,
    x_send,
    x_recv,
    x_own,
    xn_all,
    d_twin,
    d_send,
    d_recv,
    wsem,
    ssem,
    rsem,
):
    f32, bf16 = jnp.float32, jnp.bfloat16
    me = lax.axis_index("tp")
    grp = lax.axis_index("cb")
    rows, feat = hid.shape
    per_dev = rows // ntp
    heads = feat // HEAD_DIM
    blk = per_dev * heads
    steps = w_in.shape[0]
    drows = frame.shape[0] * rows // ntp
    dfeat = DD // ntp
    order = sorted(range(1, ntp), key=lambda i: abs(i - ntp // 2))
    chips = ntp // 2
    core = lax.rem(me, 2)
    chip = lax.div(me, 2)
    twin = chip * 2 + 1 - core
    far = sorted(range(1, chips), key=lambda j: abs(j - chips // 2))

    weights = {}

    def load(name, source, target, index):
        copy = pltpu.make_async_copy(source, target, wsem.at[index])
        copy.start()
        weights[name] = copy


    sent = []

    def put(source, target, phase, i, axis, device):
        copy = pltpu.make_async_remote_copy(
            src_ref=source,
            dst_ref=target,
            send_sem=ssem.at[phase, i],
            recv_sem=rsem.at[phase, i],
            device_id={axis: device},
            device_id_type=MESH,
        )
        copy.start()
        sent.append(copy)
        return copy

    def tp_at(i):
        return lax.rem(me + i, ntp)

    def cb_at(i):
        return lax.rem(grp + i, ncb)

    def same_core(j):
        return lax.rem(chip + j, chips) * 2 + core

    def share(buffers, phases):
        direct = [
            [put(b.at[me], b.at[me], p, j, "tp", same_core(j)) for b, p in zip(buffers, phases)]
            for j in far
        ]
        passed = [put(b.at[me], b.at[me], p, chips, "tp", twin) for b, p in zip(buffers, phases)]
        return direct, passed

    def pass_on(buffers, phases, state):
        direct, passed = state
        for j, copies in zip(far, direct):
            origin = same_core(chips - j)
            for b, p, copy in zip(buffers, phases, copies):
                copy.wait_recv()
                passed.append(put(b.at[origin], b.at[origin], p, chips + j, "tp", twin))
        return passed

    barrier = pltpu.get_barrier_semaphore()
    for i in range(1, ntp):
        pl.semaphore_signal(barrier, inc=1, device_id={"tp": tp_at(i)}, device_id_type=MESH)
    for i in range(1, ncb):
        pl.semaphore_signal(barrier, inc=1, device_id={"cb": cb_at(i)}, device_id_type=MESH)

    def part_of(device):
        return pl.ds(pl.multiple_of(device * feat, feat), feat)

    visits = [me, twin]
    visits += [same_core(chips - j) for j in far]
    visits += [same_core(chips - j) + 1 - 2 * core for j in far]
    for n, origin in enumerate(visits):
        load(
            ("q", n), w_qkv.at[:, part_of(origin), :], vq.at[:, part_of(origin), :], n
        )
    gain32 = gain[...].reshape(1, feat).astype(f32)
    gain_rows = [gain32[:, h * HEAD_DIM : (h + 1) * HEAD_DIM] for h in range(heads)]
    gain_rows.append(jnp.zeros((16 - heads, HEAD_DIM), f32))
    gain_all[me] = jnp.concatenate(gain_rows, axis=0).astype(bf16)
    hid_all[me] = hid[...]
    pl.semaphore_wait(barrier, ntp - 1 + ncb - 1)

    buffers, phases = [hid_all, gain_all], [NORM, GAIN]
    direct, passed = share(buffers, phases)
    relayed = []
    total = jnp.zeros((rows, 1), f32)

    size = rows * heads
    place = lax.broadcasted_iota(jnp.int32, (size, size), 0)
    column = lax.broadcasted_iota(jnp.int32, (size, size), 1)
    source = ((place // per_dev) % heads) * rows + (place // blk) * per_dev + place % per_dev
    perm = (column == source).astype(f32).astype(bf16)
    for n, origin in enumerate(visits):
        if n == 1:
            for copy in passed:
                copy.wait_recv()
        elif 2 <= n < 1 + chips:
            relayed.append([])
            for b, p, copy in zip(buffers, phases, direct[n - 2]):
                copy.wait_recv()
                relayed[-1].append(
                    put(b.at[origin], b.at[origin], p, chips + far[n - 2], "tp", twin)
                )
        elif n >= 1 + chips:
            for copy in relayed[n - 1 - chips]:
                copy.wait_recv()
        piece = hid_all[origin].astype(f32)
        gains = gain_all[origin].astype(f32)
        total = total + jnp.sum(piece * piece, axis=1, keepdims=True)
        scaled = jnp.concatenate(
            [
                piece[:, h * HEAD_DIM : (h + 1) * HEAD_DIM] * gains[h : h + 1, :]
                for h in range(heads)
            ],
            axis=1,
        ).astype(bf16)
        weights["q", n].wait()
        if n == 4:
            load("e", embed, ve, ntp)
            load("k", keys, vk, ntp + 1)
            load("v", values, vv, ntp + 2)
        if n == 6:
            load("o", w_out, vo, ntp + 3)
            load("i", w_in, vi, ntp + 4)
            load("g", w_gu, vg, ntp + 5)
            load("d", w_down, vd, ntp + 6)
        inv = lax.rsqrt(total / D + eps)
        for i in range(3):
            term = jnp.dot(scaled, vq[i, part_of(origin), :], preferred_element_type=f32)
            if n:
                term = term + acc[i]
            if n < ntp - 1:
                acc[i] = term
                continue
            full = (term * inv).astype(bf16)
            stacked = jnp.concatenate(
                [full[:, h * HEAD_DIM : (h + 1) * HEAD_DIM] for h in range(heads)], axis=0
            )
            moved = jnp.dot(perm, stacked, preferred_element_type=f32).astype(bf16)
            qkv_send[i] = moved.reshape(ntp, blk, HEAD_DIM)
    arriving = [
        put(qkv_send.at[:, tp_at(j)], qkv_recv.at[:, me], QKV, j, "tp", tp_at(j)) for j in order
    ]
    qkv_recv[:, me] = qkv_send[:, me]

    weights["e"].wait()
    codes = lax.broadcasted_iota(jnp.int32, (tokens.shape[1], CARD), 1)

    def embed_tokens(local):
        spread = jnp.broadcast_to(tokens[local : local + 1, :], (128, tokens.shape[1]))
        chosen = jnp.transpose(spread)[:, 0:1]
        one_hot = (chosen == codes).astype(f32).astype(bf16)
        emb[local] = jnp.dot(one_hot, ve[local], preferred_element_type=f32).astype(bf16)

    embed_tokens(steps - 1)
    carry = put(emb.at[steps - 1], carried, CARRY, 1, "cb", cb_at(1))
    weights["k"].wait()
    weights["v"].wait()
    for copy in arriving:
        copy.wait_recv()

    scale = 1.0 / math.sqrt(HEAD_DIM)
    slots = per_dev * CACHE
    lanes = ntp * blk
    row = lax.broadcasted_iota(jnp.int32, (lanes, slots), 0)
    col = lax.broadcasted_iota(jnp.int32, (lanes, slots), 1)
    count = jnp.zeros((lanes, slots), jnp.int32)
    for r in range(per_dev):
        count = jnp.where(col // CACHE == r, lengths[r], count)
    live = (row % per_dev == col // CACHE) & (col % CACHE < count)
    head_of = lax.broadcasted_iota(jnp.int32, (lanes, HEAD_DIM), 0) // per_dev % heads
    query = qkv_recv[0].reshape(lanes, HEAD_DIM).astype(f32)
    key_new = qkv_recv[1].reshape(lanes, HEAD_DIM).astype(f32)
    value_new = qkv_recv[2].reshape(lanes, HEAD_DIM).astype(f32)
    spread = jnp.concatenate(
        [jnp.where(head_of == h, query, 0.0) for h in range(heads)], axis=1
    ).astype(bf16)
    products = []
    for s in range(ntp):
        old_keys = vk[:, :, s * feat : (s + 1) * feat].reshape(slots, feat)
        products.append(
            lax.dot_general(
                old_keys,
                spread[s * blk : (s + 1) * blk, :],
                (((1,), (1,)), ((), ())),
                preferred_element_type=f32,
            )
        )
    scores = jnp.transpose(jnp.concatenate(products, axis=1)) * scale
    scores = jnp.where(live, scores, -1e30)
    fresh = jnp.sum(query * key_new, axis=1, keepdims=True) * scale
    top = jnp.maximum(jnp.max(scores, axis=1, keepdims=True), fresh)
    weight = jnp.exp(scores - top)
    weight_new = jnp.exp(fresh - top)
    norm = jnp.sum(weight, axis=1, keepdims=True) + weight_new
    probs = (weight / norm).astype(bf16)
    mixed_new = (weight_new / norm).astype(bf16).astype(f32) * value_new
    for s in range(ntp):
        mine = slice(s * blk, (s + 1) * blk)
        old_values = vv[:, :, s * feat : (s + 1) * feat].reshape(slots, feat)
        wide = jnp.dot(probs[mine, :], old_values, preferred_element_type=f32)
        mixed = mixed_new[mine, :]
        for h in range(heads):
            mixed = mixed + jnp.where(
                head_of[mine, :] == h, wide[:, h * HEAD_DIM : (h + 1) * HEAD_DIM], 0.0
            )
        att_send[s] = mixed.astype(bf16)
    arriving = [
        put(att_send.at[tp_at(i)], att_recv.at[me], BACK, i, "tp", tp_at(i)) for i in order
    ]
    att_recv[me] = att_send[me]
    for copy in arriving:
        copy.wait_recv()
    gathered = att_recv[...].reshape(ntp * blk, HEAD_DIM)
    place = lax.broadcasted_iota(jnp.int32, (rows, ntp * blk), 0)
    column = lax.broadcasted_iota(jnp.int32, (rows, ntp * blk), 1)
    for h in range(heads):
        source = (place // per_dev) * blk + h * per_dev + place % per_dev
        pick = (column == source).astype(f32).astype(bf16)
        returned[:, h * HEAD_DIM : (h + 1) * HEAD_DIM] = jnp.dot(
            pick, gathered, preferred_element_type=f32
        ).astype(bf16)

    weights["o"].wait()

    def projected(device):
        cols = pl.ds(pl.multiple_of(device * feat, feat), feat)
        return jnp.dot(returned[...], vo[:, cols], preferred_element_type=f32)

    for z in range(chips):
        o_twin[0, z] = projected(2 * z + 1 - core).astype(bf16)
    merged = put(o_twin.at[0], o_twin.at[1], OUT, 0, "tp", twin)
    mine = [projected(same_core(j)) for j in far + [0]]
    merged.wait_recv()
    arriving = []
    for j, term in zip(far, mine):
        o_send[j] = (term + o_twin[1, lax.rem(chip + j, chips)].astype(f32)).astype(bf16)
        arriving.append(put(o_send.at[j], o_recv.at[j], OUT, j, "tp", same_core(j)))
    attn = mine[-1] + o_twin[1, chip].astype(f32)
    for j, copy in zip(far, arriving):
        copy.wait_recv()
        attn = attn + o_recv[j].astype(f32)
    temporal = (hid[...].astype(f32) + attn).astype(bf16)
    out_t[...] = temporal
    frame[grp] = temporal

    arriving = [
        put(frame.at[grp], frame.at[grp], FRAME, i, "cb", cb_at(i)) for i in range(1, ncb)
    ]
    for local in range(steps - 1):
        embed_tokens(local)
    weights["i"].wait()
    carry.wait_recv()
    for copy in arriving:
        copy.wait_recv()
    lhs = frame[...].reshape(ncb * rows, feat)

    own_cols = pl.ds(pl.multiple_of(me * dfeat, dfeat), dfeat)

    def rows_of(device):
        return pl.ds(pl.multiple_of(device * drows, drows), drows)

    def cols_of(device):
        return pl.ds(pl.multiple_of(device * dfeat, dfeat), dfeat)

    merged, arriving = [], []

    def send_input(local):
        merged[local].wait_recv()
        copies = []
        for j in far:
            x_send[local, j] = (
                part[local, rows_of(same_core(j)), :]
                + x_twin[local, 1, lax.rem(chip + j, chips)].astype(f32)
            ).astype(bf16)
            copies.append(
                put(x_send.at[local, j], x_recv.at[local, j], XSUM + local, j, "tp", same_core(j))
            )
        arriving.append(copies)

    for local in range(steps):
        part[local] = jnp.dot(lhs, vi[local], preferred_element_type=f32)
        before = carried[...] if local == 0 else emb[local - 1]
        part[local, :, own_cols] = part[local, :, own_cols] + before.astype(f32)
        if local:
            send_input(local - 1)
        for z in range(chips):
            x_twin[local, 0, z] = part[local, rows_of(2 * z + 1 - core), :].astype(bf16)
        merged.append(
            put(x_twin.at[local, 0], x_twin.at[local, 1], XSUM + local, 0, "tp", twin)
        )
    send_input(steps - 1)
    gathers = []
    for local in range(steps):
        x = part[local, rows_of(me), :] + x_twin[local, 1, chip].astype(f32)
        for j, copy in zip(far, arriving[local]):
            copy.wait_recv()
            x = x + x_recv[local, j].astype(f32)
        x_own[local] = x
        inv = lax.rsqrt(jnp.sum(x * x, axis=1, keepdims=True) / DD + eps)
        gains = depth_gain[local : local + 1, :].astype(f32)
        xn_all[local, me] = (x * inv * gains).astype(bf16)
        gathers.append(share([xn_all.at[local]], [XN + local]))

    weights["g"].wait()
    weights["d"].wait()
    contract_last = (((1,), (1,)), ((), ()))
    gathers[0] = pass_on([xn_all.at[0]], [XN], gathers[0])
    merged, summed = [], []

    def send_down(local):
        merged[local].wait_recv()
        copies = []
        for j in far:
            d_send[local, j] = (
                part[local, :, cols_of(same_core(j))]
                + d_twin[local, 1, lax.rem(chip + j, chips)].astype(f32)
            ).astype(bf16)
            copies.append(
                put(d_send.at[local, j], d_recv.at[local, j], DOWN + local, j, "tp", same_core(j))
            )
        summed.append(copies)

    for local in range(steps):
        for copy in gathers[local]:
            copy.wait_recv()
        lhs = xn_all[local].reshape(ntp * drows, DD)
        gate = lax.dot_general(vg[local, 0], lhs, contract_last, preferred_element_type=f32)
        upper = lax.dot_general(vg[local, 1], lhs, contract_last, preferred_element_type=f32)
        act = jnp.transpose(jax.nn.silu(gate) * upper).astype(bf16)
        if local + 1 < steps:
            gathers[local + 1] = pass_on(
                [xn_all.at[local + 1]], [XN + local + 1], gathers[local + 1]
            )
        if local:
            send_down(local - 1)
        part[local] = jnp.dot(act, vd[local], preferred_element_type=f32)
        part[local, rows_of(me), :] = part[local, rows_of(me), :] + x_own[local]
        for z in range(chips):
            d_twin[local, 0, z] = part[local, :, cols_of(2 * z + 1 - core)].astype(bf16)
        merged.append(
            put(d_twin.at[local, 0], d_twin.at[local, 1], DOWN + local, 0, "tp", twin)
        )
    send_down(steps - 1)
    early = len(sent) - len(far) * steps
    for copy in sent[:early]:
        copy.wait_send()
    for local in range(steps):
        y = part[local, :, own_cols] + d_twin[local, 1, chip].astype(f32)
        for j, copy in zip(far, summed[local]):
            copy.wait_recv()
            y = y + d_recv[local, j].astype(f32)
        out_d[local] = y.astype(out_d.dtype)
    for copy in sent[early:]:
        copy.wait_send()


def finish(temporal, depth, out_t, out_d):
    out_t[...] = temporal[...]
    out_d[...] = depth[...]


def fits(mesh, hidden_in, w_in):
    ntp, ncb = mesh.shape["tp"], mesh.shape["cb"]
    rows, feat = hidden_in.shape[0] // ncb, hidden_in.shape[1] // ntp
    steps = w_in.shape[0] // ncb
    return (
        steps == 2
        and ntp % 2 == 0
        and rows * ncb == 128
        and ntp == 8
        and feat % HEAD_DIM == 0
        and feat // HEAD_DIM <= 16
        and rows % ntp == 0
        and (rows // ntp * (feat // HEAD_DIM)) % 16 == 0
        and (rows * ncb) % (16 * ntp) == 0
        and (DD // ntp) % 128 == 0
    )


def fused(
    hidden_in,
    norm_gain,
    w_qkv,
    w_out,
    cache_keys,
    cache_values,
    lengths,
    tokens,
    w_in,
    embed,
    depth_gain,
    w_gate_up,
    w_down,
):
    ntp, ncb = lax.axis_size("tp"), lax.axis_size("cb")
    f32, bf16 = jnp.float32, jnp.bfloat16
    rows, feat = hidden_in.shape
    blk = rows // ntp * (feat // HEAD_DIM)
    steps = w_in.shape[0]
    chips = ntp // 2
    total_rows = rows * ncb
    drows, dfeat = total_rows // ntp, DD // ntp
    vmem = pl.BlockSpec(memory_space=pltpu.VMEM)
    hbm = pl.BlockSpec(memory_space=pl.ANY)
    big = [w_qkv, w_out, cache_keys, cache_values, w_in, embed, jnp.swapaxes(w_gate_up, 2, 3), w_down]
    scratch = [pltpu.VMEM(a.shape, a.dtype) for a in big] + [
        pltpu.VMEM((ntp, rows, feat), bf16),
        pltpu.VMEM((ntp, 16, HEAD_DIM), bf16),
        pltpu.VMEM((3, rows, feat), f32),
        pltpu.VMEM((3, ntp, blk, HEAD_DIM), bf16),
        pltpu.VMEM((3, ntp, blk, HEAD_DIM), bf16),
        pltpu.VMEM((ntp, blk, HEAD_DIM), bf16),
        pltpu.VMEM((ntp, blk, HEAD_DIM), bf16),
        pltpu.VMEM((rows, feat), bf16),
        pltpu.VMEM((2, chips, rows, feat), bf16),
        pltpu.VMEM((chips, rows, feat), bf16),
        pltpu.VMEM((chips, rows, feat), bf16),
        pltpu.VMEM((ncb, rows, feat), bf16),
        pltpu.VMEM((steps, total_rows, dfeat), bf16),
        pltpu.VMEM((total_rows, dfeat), bf16),
        pltpu.VMEM((steps, total_rows, DD), f32),
        pltpu.VMEM((steps, 2, chips, drows, DD), bf16),
        pltpu.VMEM((steps, chips, drows, DD), bf16),
        pltpu.VMEM((steps, chips, drows, DD), bf16),
        pltpu.VMEM((steps, drows, DD), f32),
        pltpu.VMEM((steps, ntp, drows, DD), bf16),
        pltpu.VMEM((steps, 2, chips, total_rows, dfeat), bf16),
        pltpu.VMEM((steps, chips, total_rows, dfeat), bf16),
        pltpu.VMEM((steps, chips, total_rows, dfeat), bf16),
        pltpu.SemaphoreType.DMA((ntp + 7,)),
        pltpu.SemaphoreType.DMA((PHASES, ntp)),
        pltpu.SemaphoreType.DMA((PHASES, ntp)),
    ]
    temporal, depth = pl.pallas_call(
        functools.partial(frame_kernel, ntp, ncb),
        out_shape=(
            jax.ShapeDtypeStruct((rows, feat), bf16),
            jax.ShapeDtypeStruct((steps, total_rows, dfeat), bf16),
        ),
        in_specs=[vmem, vmem, pl.BlockSpec(memory_space=pltpu.SMEM), vmem, vmem] + [hbm] * 8,
        out_specs=(vmem, vmem),
        scratch_shapes=scratch,
        compiler_params=pltpu.CompilerParams(
            collective_id=0, has_side_effects=True, vmem_limit_bytes=60 * 1024 * 1024
        ),
    )(
        hidden_in,
        norm_gain,
        lengths,
        tokens.T,
        depth_gain,
        *big,
    )
    return pl.pallas_call(
        finish,
        out_shape=(
            jax.ShapeDtypeStruct(temporal.shape, bf16),
            jax.ShapeDtypeStruct(depth.shape, bf16),
        ),
        in_specs=[vmem, vmem],
        out_specs=(vmem, vmem),
    )(temporal, depth)


def solution(mesh):
    in_specs = (
        P("cb", "tp"),
        P("tp"),
        P(None, None, "tp"),
        P("tp", None),
        P(("cb", "tp"), None, None),
        P(("cb", "tp"), None, None),
        P(("cb", "tp")),
        P(None, "cb"),
        P("cb", "tp", None),
        P("cb", None, "tp"),
        P("cb", None),
        P("cb", None, None, "tp"),
        P("cb", "tp", None),
    )
    out_specs = (P("cb", "tp"), P("cb", None, "tp"))

    def run(*args):
        body = fused if fits(mesh, args[0], args[8]) else per_device
        return jax.shard_map(
            body, mesh=mesh, in_specs=in_specs, out_specs=out_specs, check_vma=False
        )(*args)

    return run
```
